128 devices in a mesh: dp: 8 (over x, core), shard: 16 (over y, z).
Axes of the slice: x: 4, y: 4, z: 4, core: 2. Of those that a mesh axis runs over, the one named last changes fastest.
Arguments:
- inputs: bfloat16 [98304, 7168], P(('dp', 'shard')), may hold values from -80 to 80, as said below
- cotangent: bfloat16 [98304, 512], P(('dp', 'shard')), may hold values from -20 to 20
- weight: bfloat16 [7168, 512], P('shard'), may hold values from -1 to 1
- norm_gain: float32 [512], replicated, may hold values from 0.25 to 1.75
Outputs:
- input_grad: bfloat16 [98304, 7168], P(('dp', 'shard'))
- weight_grad: float32 [7168, 512], P(('dp', 'shard'))
- gain_grad: float32 [512], replicated
The draws below stay inside these ranges and needn't reach their ends.
Inputs may be any that keep to these rules, and one draw needn't show every extreme that they name: `inputs`: activations with per-token scales.
All inputs are finite; a program needn't handle non-finite values.
Results may differ from the reference program's by a relative error of at most 0.0049.
Values may be sent and summed in bfloat16 or wider, within the bound.
No kernel may reach another device: no remote copies, remote signals or barrier semaphores. Data moves between devices by JAX's collectives and lax.ppermute only.
A program may use at most 128 MiB of HBM per device.

```python
import math
import jax
import jax.numpy as jnp
from jax import lax

D = 7168
KVR = 512
TOKENS = 98304


def draw_inputs(key, part):
    key = jax.random.fold_in(key, 11)
    first, second = jax.random.split(key, 2)
    row_scale = jnp.exp(jax.random.uniform(first, (TOKENS, 1), jnp.float32) * math.log(10.0))
    values = jax.random.normal(second, (TOKENS, D), jnp.float32)
    return (values * row_scale).astype(jnp.bfloat16)


def draw_cotangent(key, part):
    key = jax.random.fold_in(key, 23)
    position = jnp.arange(TOKENS, dtype=jnp.float32)[:, None] / max(TOKENS - 1, 1)
    rising = 1.0 + 2.0 * position
    values = jnp.clip(jax.random.normal(key, (TOKENS, KVR), jnp.float32), -6.0, 6.0) * rising
    return values.astype(jnp.bfloat16)


def draw_weight(key, part):
    key = jax.random.fold_in(key, 37)
    first, second = jax.random.split(key)
    column_scale = jnp.exp(jax.random.uniform(first, (1, KVR), jnp.float32, math.log(0.3), math.log(3.0)))
    values = jax.random.normal(second, (D, KVR), jnp.float32)
    return (values * column_scale / math.sqrt(D)).astype(jnp.bfloat16)


def setup_inputs(seed: int = 0) -> dict:
    splits = jax.random.split(jax.random.key(seed), 5)
    return {
        "inputs": draw_inputs(jax.random.fold_in(splits[4], 71), 0),
        "cotangent": draw_cotangent(jax.random.fold_in(splits[4], 71), 0),
        "weight": draw_weight(jax.random.fold_in(splits[4], 71), 0),
        "norm_gain": jnp.clip(1.0 + 0.15 * jax.random.normal(splits[3], (KVR,), jnp.float32), 0.25, 1.75),
    }


epsilon = 1e-06

def reference(inputs, cotangent, weight, norm_gain):
    latent = jnp.dot(inputs, weight, preferred_element_type=jnp.float32)
    inverse_scale = lax.rsqrt(lax.optimization_barrier(jnp.mean(latent * latent, axis=-1, keepdims=True)) + epsilon)
    normed = latent * inverse_scale
    upstream = cotangent.astype(jnp.float32)
    gain_grad = lax.optimization_barrier(jnp.sum(upstream * normed, axis=0))
    scaled = upstream * norm_gain.astype(jnp.float32)
    center = lax.optimization_barrier(jnp.mean(scaled * normed, axis=-1, keepdims=True))
    latent_grad = (inverse_scale * (scaled - normed * center)).astype(jnp.bfloat16)
    input_grad = jnp.dot(latent_grad, weight.T, preferred_element_type=jnp.float32).astype(jnp.bfloat16)
    weight_grad = jnp.dot(inputs.T, latent_grad, preferred_element_type=jnp.float32)
    return (input_grad, weight_grad, gain_grad)
```

```python
import jax
import jax.numpy as jnp
from jax import lax
from jax.sharding import PartitionSpec as P

epsilon = 1e-06
axes = ("dp", "shard")


def device(x, core, y, z):
    return ((x % 4) * 2 + core) * 16 + (y % 4) * 4 + z % 4


def permute(value, move):
    pairs = [
        (device(x, c, y, z), device(*move(x, c, y, z)))
        for x in range(4)
        for c in range(2)
        for y in range(4)
        for z in range(4)
    ]
    return lax.ppermute(value, axes, pairs)


def twin(value):
    return permute(value, lambda x, c, y, z: (x, 1 - c, y, z))


def shift(value, axis, by):
    step = [by if axis == name else 0 for name in "xyz"]
    return permute(value, lambda x, c, y, z: (x + step[0], c, y + step[1], z + step[2]))


def pick(value, index):
    return lax.dynamic_index_in_dim(value, index % 4, 0, keepdims=False)


def reduce_over(value, axis, position):
    own = pick(value, position).astype(jnp.float32)
    near = [shift(pick(value, position + by), axis, by).astype(jnp.float32) for by in (1, 2, 3)]
    return (own + near[1]) + (near[0] + near[2])


def sum_over(value, axis):
    near = [shift(value, axis, by) for by in (1, 2, 3)]
    return (value + near[1]) + (near[0] + near[2])


def shards(inputs, cotangent, weight, norm_gain):
    dp, shard = lax.axis_index("dp"), lax.axis_index("shard")
    place = {"x": dp // 2, "y": shard // 4, "z": shard % 4}
    core = dp % 2
    half = lax.dynamic_slice_in_dim(weight, core * 224, 224, 0)
    mine = lax.all_gather(half, "shard", axis=0, tiled=False)
    other = twin(mine)
    gathered = jnp.where(core == 0, jnp.stack([mine, other], 1), jnp.stack([other, mine], 1))
    gathered = gathered.reshape(7168, 512)
    latent = jnp.dot(inputs, gathered, preferred_element_type=jnp.float32)
    inverse_scale = lax.rsqrt(jnp.mean(latent * latent, axis=-1, keepdims=True) + epsilon)
    normed = latent * inverse_scale
    upstream = cotangent.astype(jnp.float32)
    gain_grad = jnp.sum(upstream * normed, axis=0)
    gain_grad = gain_grad + twin(gain_grad)
    for axis in "xyz":
        gain_grad = sum_over(gain_grad, axis)
    scaled = upstream * norm_gain
    center = jnp.mean(scaled * normed, axis=-1, keepdims=True)
    latent_grad = (inverse_scale * (scaled - normed * center)).astype(jnp.bfloat16)
    input_grad = lax.dot_general(
        latent_grad, gathered, (((1,), (1,)), ((), ())), preferred_element_type=jnp.float32
    )
    input_grad = input_grad.astype(jnp.bfloat16)
    partial = lax.dot_general(
        inputs, latent_grad, (((0,), (0,)), ((), ())), preferred_element_type=jnp.float32
    ).astype(jnp.bfloat16)
    partial = partial.reshape(4, 2, 4, 4, 56, 512)
    kept = lax.dynamic_index_in_dim(partial, core, 1, keepdims=False)
    sent = lax.dynamic_index_in_dim(partial, 1 - core, 1, keepdims=False)
    both = (kept.astype(jnp.float32) + twin(sent).astype(jnp.float32)).astype(jnp.bfloat16)
    pieces = []
    for start, stop, order in ((0, 24, "xyz"), (24, 40, "yzx"), (40, 56, "zxy")):
        piece = both[:, :, :, start:stop]
        left = "xyz"
        for axis in order:
            piece = jnp.moveaxis(piece, left.index(axis), 0)
            piece = reduce_over(piece, axis, place[axis])
            left = left.replace(axis, "")
            if left:
                piece = piece.astype(jnp.bfloat16)
        pieces.append(piece)
    weight_grad = jnp.concatenate(pieces, 0)
    return (input_grad, weight_grad, gain_grad)


def solution(mesh):
    placed = (P(("dp", "shard"), None), P(("dp", "shard"), None), P("shard", None), P())
    return jax.shard_map(
        shards,
        mesh=mesh,
        in_specs=placed,
        out_specs=(P(("dp", "shard"), None), P(("dp", "shard"), None), P()),
        check_vma=False,
    )
```

```python
import jax
import jax.numpy as jnp
from jax import lax
from jax.sharding import PartitionSpec as P

epsilon = 1e-06
axes = ("dp", "shard")


def device(x, core, y, z):
    return (x * 2 + core) * 16 + y * 4 + z


four = range(4)
along_y = [[y * 4 + z for y in four] for z in four]
along_z = [[y * 4 + z for z in four] for y in four]
chips = [[device(x, c, y, z) for x in four for y in four for z in four] for c in range(2)]
cores = [(device(x, c, y, z), device(x, 1 - c, y, z)) for x in four for c in range(2) for y in four for z in four]


def twin(value):
    return lax.ppermute(value, axes, cores)


def gather(value, groups):
    copies = jnp.broadcast_to(value[None], (4,) + value.shape)
    return lax.all_to_all(copies, "shard", 0, 0, axis_index_groups=groups, tiled=True)


def shards(inputs, cotangent, weight, norm_gain):
    core = lax.axis_index("dp") % 2
    half = lax.dynamic_slice_in_dim(weight, core * 224, 224, 0)
    first = gather(gather(half[:112], along_y), along_z)
    second = gather(gather(half[112:], along_z), along_y)
    mine = jnp.stack([first.swapaxes(0, 1), second], 2)
    other = twin(mine)
    gathered = jnp.where(core == 0, jnp.stack([mine, other], 2), jnp.stack([other, mine], 2))
    gathered = gathered.reshape(7168, 512)
    latent = jnp.dot(inputs, gathered, preferred_element_type=jnp.float32)
    inverse_scale = lax.rsqrt(jnp.mean(latent * latent, axis=-1, keepdims=True) + epsilon)
    normed = latent * inverse_scale
    upstream = cotangent.astype(jnp.float32)
    gain_grad = jnp.sum(upstream * normed, axis=0)
    gain_grad = jnp.broadcast_to(gain_grad.reshape(1, 4, 128), (128, 4, 128))
    gain_grad = lax.all_to_all(gain_grad, axes, 0, 0, tiled=True)
    gain_grad = jnp.sum(gain_grad, axis=0).reshape(512)
    scaled = upstream * norm_gain
    center = jnp.mean(scaled * normed, axis=-1, keepdims=True)
    latent_grad = (inverse_scale * (scaled - normed * center)).astype(jnp.bfloat16)
    partial = lax.dot_general(
        inputs, latent_grad, (((0,), (0,)), ((), ())), preferred_element_type=jnp.float32
    ).astype(jnp.bfloat16)
    partial = partial.reshape(4, 2, 16, 56, 512)
    kept = lax.dynamic_index_in_dim(partial, core, 1, keepdims=False)
    sent = lax.dynamic_index_in_dim(partial, 1 - core, 1, keepdims=False)
    both = (kept.astype(jnp.float32) + twin(sent).astype(jnp.float32)).astype(jnp.bfloat16)
    pieces = lax.all_to_all(both.reshape(64, 56, 512), axes, 0, 0, axis_index_groups=chips, tiled=True)
    weight_grad = jnp.sum(pieces.astype(jnp.float32), axis=0)
    input_grad = lax.dot_general(
        latent_grad, gathered, (((1,), (1,)), ((), ())), preferred_element_type=jnp.float32
    )
    return (input_grad.astype(jnp.bfloat16), weight_grad, gain_grad)


def solution(mesh):
    placed = (P(("dp", "shard"), None), P(("dp", "shard"), None), P("shard", None), P())
    return jax.shard_map(
        shards,
        mesh=mesh,
        in_specs=placed,
        out_specs=(P(("dp", "shard"), None), P(("dp", "shard"), None), P()),
        check_vma=False,
    )
```

```python
import jax
import jax.numpy as jnp
from jax import lax
from jax.experimental import pallas as pl
from jax.experimental.pallas import tpu as pltpu
from jax.sharding import PartitionSpec as P

epsilon = 1e-06
axes = ("dp", "shard")
bf16, f32 = jnp.bfloat16, jnp.float32
MIB = 1024 * 1024


def device(x, core, y, z):
    return ((x % 4) * 2 + core) * 16 + (y % 4) * 4 + z % 4


four = range(4)
spots = [(x, c, y, z) for x in four for c in range(2) for y in four for z in four]
chips = [[device(x, c, y, z) for x in four for y in four for z in four] for c in range(2)]


def fetch(value, source):
    return lax.ppermute(value, axes, [(device(*source(*spot)), device(*spot)) for spot in spots])


def twin(value):
    return fetch(value, lambda x, c, y, z: (x, 1 - c, y, z))


def fetch_first(value, by):
    return fetch(value, lambda x, c, y, z: (x, c, y, z + by) if c else (x, c, y + by, z))


def fetch_second(value, by):
    return fetch(value, lambda x, c, y, z: (x, c, y + by, z) if c else (x, c, y, z + by))


def turn_kernel(place, kept, sent, after, kept_out, sent_out):
    for column in range(0, 896, 128):
        kept_out[column : column + 128, :] = kept[:, column : column + 128].T
        sent_out[column : column + 128, :] = sent[:, column : column + 128].T


def turn(place, inputs, after):
    return pl.pallas_call(
        turn_kernel,
        grid_spec=pltpu.PrefetchScalarGridSpec(
            num_scalar_prefetch=1,
            grid=(4,),
            in_specs=[
                pl.BlockSpec((768, 896), lambda i, place: (0, 2 * i + place[1])),
                pl.BlockSpec((768, 896), lambda i, place: (0, 2 * i + 1 - place[1])),
                pl.BlockSpec(memory_space=pl.ANY),
            ],
            out_specs=[pl.BlockSpec((896, 768), lambda i, place: (i, 0))] * 2,
        ),
        out_shape=[jax.ShapeDtypeStruct((3584, 768), bf16)] * 2,
        compiler_params=pltpu.CompilerParams(vmem_limit_bytes=24 * MIB),
        cost_estimate=pl.CostEstimate(flops=0, bytes_accessed=44 * MIB, transcendentals=0),
        name="turn",
    )(place, inputs, inputs, after)


def latent_kernel(place, inputs, cotangent, gain, *rest):
    pieces, (out, weight_out, held, leave) = rest[:8], rest[8:]
    step = pl.program_id(0)
    core, y, z = place[1], place[2], place[3]
    copy = pltpu.make_async_copy(held, weight_out, leave)

    @pl.when(step == 0)
    def _():
        for side in range(2):
            part = core if side == 0 else 1 - core
            for far in four:
                for near in four:
                    along_y = lax.rem(y + jnp.where(part == 0, near, far), 4)
                    along_z = lax.rem(z + jnp.where(part == 0, far, near), 4)
                    start = pl.multiple_of((along_y * 4 + along_z) * 448 + part * 224, 224)
                    held[pl.ds(start, 224), :] = pieces[side * 4 + far][near]
        copy.start()

    latent = jnp.dot(inputs[...], held[...], preferred_element_type=f32)
    scale = lax.rsqrt(jnp.mean(latent * latent, axis=1, keepdims=True) + epsilon)
    normed = latent * scale
    upstream = cotangent[...].astype(f32)
    scaled = upstream * gain[...]
    center = jnp.mean(scaled * normed, axis=1, keepdims=True)
    out[pl.ds(pl.multiple_of(step * 256, 256), 256), :] = (scale * (scaled - normed * center)).astype(bf16)
    gain_grad = jnp.sum(upstream * normed, axis=0, keepdims=True)

    @pl.when(step > 0)
    def _():
        out_gain = gain_grad + total_of(out)
        out[768:784, :] = split(out_gain)

    @pl.when(step == 0)
    def _():
        out[768:784, :] = split(gain_grad)

    @pl.when(step == 2)
    def _():
        copy.wait()


def split(value):
    high = value.astype(bf16).astype(f32)
    middle = (value - high).astype(bf16).astype(f32)
    low = value - high - middle
    return jnp.concatenate([high, middle, low, jnp.zeros((13, 512), f32)], axis=0).astype(bf16)


def total_of(rows):
    return jnp.sum(rows[768:784, :].astype(f32), axis=0, keepdims=True)


def latent_grads(place, inputs, cotangent, gain, pieces):
    return pl.pallas_call(
        latent_kernel,
        grid_spec=pltpu.PrefetchScalarGridSpec(
            num_scalar_prefetch=1,
            grid=(3,),
            in_specs=[
                pl.BlockSpec((256, 7168), lambda i, place: (i, 0)),
                pl.BlockSpec((256, 512), lambda i, place: (i, 0)),
                pl.BlockSpec((1, 512), lambda i, place: (0, 0)),
            ]
            + [pl.BlockSpec(memory_space=pltpu.VMEM)] * 8,
            out_specs=[
                pl.BlockSpec((784, 512), lambda i, place: (0, 0)),
                pl.BlockSpec(memory_space=pl.ANY),
            ],
            scratch_shapes=[pltpu.VMEM((7168, 512), bf16), pltpu.SemaphoreType.DMA],
        ),
        out_shape=[jax.ShapeDtypeStruct((784, 512), bf16), jax.ShapeDtypeStruct((7168, 512), bf16)],
        compiler_params=pltpu.CompilerParams(vmem_limit_bytes=40 * MIB),
        cost_estimate=pl.CostEstimate(flops=2 * 768 * 7168 * 512, bytes_accessed=28 * MIB, transcendentals=768),
        name="latent",
    )(place, inputs, cotangent, gain, *pieces)


def weight_kernel(mine, other, mine_grad, other_grad, out):
    product = jnp.dot(mine[...], mine_grad[:768, :], preferred_element_type=f32)
    product += jnp.dot(other[...], other_grad[:768, :], preferred_element_type=f32)
    pair = total_of(mine_grad) + total_of(other_grad)
    high = pair.astype(bf16).astype(f32)
    middle = (pair - high).astype(bf16).astype(f32)
    low = pair - high - middle
    lanes = [slice(128 * i, 128 * i + 128) for i in four]
    tail = [value[:, lane] for value in (high, middle, low) for lane in lanes] + [jnp.zeros((4, 128), f32)]
    for i in range(8):
        chunk = [product[56 * i : 56 * i + 56, lane] for lane in lanes]
        out[i, :, :] = jnp.concatenate(chunk + tail, axis=0).astype(bf16)


def weight_grads(mine, other, mine_grad, other_grad):
    return pl.pallas_call(
        weight_kernel,
        grid=(8,),
        in_specs=[pl.BlockSpec((448, 768), lambda i: (i, 0))] * 2 + [pl.BlockSpec((784, 512), lambda i: (0, 0))] * 2,
        out_specs=pl.BlockSpec((8, 240, 128), lambda i: (i, 0, 0)),
        out_shape=jax.ShapeDtypeStruct((64, 240, 128), bf16),
        compiler_params=pltpu.CompilerParams(vmem_limit_bytes=24 * MIB),
        cost_estimate=pl.CostEstimate(flops=2 * 768 * 7168 * 512, bytes_accessed=18 * MIB, transcendentals=0),
        name="weight_grads",
    )(mine, other, mine_grad, other_grad)


def sum_kernel(pieces, weight_grad, gain_grad):
    total = pieces[0].astype(f32)
    for i in range(1, 64):
        total = total + pieces[i].astype(f32)
    for i in four:
        weight_grad[:, 128 * i : 128 * i + 128] = total[56 * i : 56 * i + 56, :]
    gain_grad[...] = total[224:228, :] + total[228:232, :] + total[232:236, :]


def sums(pieces):
    return pl.pallas_call(
        sum_kernel,
        out_shape=[jax.ShapeDtypeStruct((56, 512), f32), jax.ShapeDtypeStruct((4, 128), f32)],
        compiler_params=pltpu.CompilerParams(vmem_limit_bytes=24 * MIB),
        name="sums",
    )(pieces)


def shards(inputs, cotangent, weight, norm_gain):
    dp, shard = lax.axis_index("dp"), lax.axis_index("shard")
    core = dp % 2
    place = jnp.stack([dp // 2, core, shard // 4, shard % 4]).astype(jnp.int32)
    half = lax.dynamic_slice_in_dim(weight, core * 224, 224, 0)
    line = jnp.stack([half] + [fetch_first(half, by) for by in (1, 2, 3)])
    mine = [line] + [fetch_second(line, by) for by in (1, 2, 3)]
    pieces = mine + [twin(piece) for piece in mine]
    kept, sent = turn(place, inputs, line)
    other = twin(sent)
    latent_grad, gathered = latent_grads(place, inputs, cotangent, norm_gain.reshape(1, 512), pieces)
    other_grad = twin(latent_grad)
    partial = weight_grads(kept, other, latent_grad, other_grad)
    partial = lax.all_to_all(partial, axes, 0, 0, axis_index_groups=chips, tiled=True)
    weight_grad, gain_grad = sums(partial)
    input_grad = lax.dot_general(
        latent_grad[:768], gathered, (((1,), (1,)), ((), ())), preferred_element_type=f32
    )
    return (input_grad.astype(bf16), weight_grad, gain_grad.reshape(512))


def solution(mesh):
    placed = (P(("dp", "shard"), None), P(("dp", "shard"), None), P("shard", None), P())
    return jax.shard_map(
        shards,
        mesh=mesh,
        in_specs=placed,
        out_specs=(P(("dp", "shard"), None), P(("dp", "shard"), None), P()),
        check_vma=False,
    )
```

```python
import jax
import jax.numpy as jnp
from jax import lax
from jax.experimental import pallas as pl
from jax.experimental.pallas import tpu as pltpu
from jax.sharding import PartitionSpec as P

epsilon = 1e-06
axes = ("dp", "shard")
bf16, f32 = jnp.bfloat16, jnp.float32
MIB = 1024 * 1024


def device(x, core, y, z):
    return ((x % 4) * 2 + core) * 16 + (y % 4) * 4 + z % 4


four = range(4)
spots = [(x, c, y, z) for x in four for c in range(2) for y in four for z in four]


def fetch(value, source):
    return lax.ppermute(value, axes, [(device(*source(*spot)), device(*spot)) for spot in spots])


def twin(value):
    return fetch(value, lambda x, c, y, z: (x, 1 - c, y, z))


def fetch_first(value, by):
    return fetch(value, lambda x, c, y, z: (x, c, y, z + by) if c else (x, c, y + by, z))


def fetch_second(value, by):
    return fetch(value, lambda x, c, y, z: (x, c, y + by, z) if c else (x, c, y, z + by))


order = jax.ShapeDtypeStruct((8, 128), f32)


def turn_kernel(place, rows, out, token):
    token[...] = jnp.zeros((8, 128), f32)
    for column in range(0, 896, 128):
        out[column : column + 128, :] = rows[:, column : column + 128].T


def turn(place, inputs):
    return pl.pallas_call(
        turn_kernel,
        grid_spec=pltpu.PrefetchScalarGridSpec(
            num_scalar_prefetch=1,
            grid=(4,),
            in_specs=[pl.BlockSpec((768, 896), lambda i, place: (0, 2 * i + place[1]))],
            out_specs=[
                pl.BlockSpec((896, 768), lambda i, place: (i, 0)),
                pl.BlockSpec((8, 128), lambda i, place: (0, 0)),
            ],
        ),
        out_shape=[jax.ShapeDtypeStruct((3584, 768), bf16), order],
        compiler_params=pltpu.CompilerParams(vmem_limit_bytes=52 * MIB),
        cost_estimate=pl.CostEstimate(flops=0, bytes_accessed=22 * MIB, transcendentals=0),
        name="turn",
    )(place, inputs)


def tie_kernel(value, token, out):
    out[...] = value[...]


def tie(value, token):
    vmem = pl.BlockSpec(memory_space=pltpu.VMEM)
    return pl.pallas_call(
        tie_kernel,
        in_specs=[vmem] * 2,
        out_specs=vmem,
        out_shape=jax.ShapeDtypeStruct(value.shape, value.dtype),
        compiler_params=pltpu.CompilerParams(vmem_limit_bytes=8 * MIB),
        cost_estimate=pl.CostEstimate(flops=0, bytes_accessed=2 * MIB, transcendentals=0),
        name="tie",
    )(value, token)


def join_kernel(one, two, three, four_, token, out):
    for i, ref in enumerate((one, two, three, four_)):
        out[i] = ref[...]


def join(values, token):
    vmem = pl.BlockSpec(memory_space=pltpu.VMEM)
    return pl.pallas_call(
        join_kernel,
        in_specs=[vmem] * 5,
        out_specs=vmem,
        out_shape=jax.ShapeDtypeStruct((4, 224, 512), bf16),
        compiler_params=pltpu.CompilerParams(vmem_limit_bytes=8 * MIB),
        cost_estimate=pl.CostEstimate(flops=0, bytes_accessed=2 * MIB, transcendentals=0),
        name="join",
    )(*values, token)


def latent_kernel(place, inputs, cotangent, gain, *rest):
    pieces, (out, weight_out, held, leave) = rest[:8], rest[8:]
    step = pl.program_id(0)
    core, y, z = place[1], place[2], place[3]
    copy = pltpu.make_async_copy(held, weight_out, leave)

    @pl.when(step == 0)
    def _():
        for side in range(2):
            part = core if side == 0 else 1 - core
            for far in four:
                for near in four:
                    along_y = lax.rem(y + jnp.where(part == 0, near, far), 4)
                    along_z = lax.rem(z + jnp.where(part == 0, far, near), 4)
                    start = pl.multiple_of((along_y * 4 + along_z) * 448 + part * 224, 224)
                    held[pl.ds(start, 224), :] = pieces[side * 4 + far][near]
        copy.start()

    latent = jnp.dot(inputs[...], held[...], preferred_element_type=f32)
    scale = lax.rsqrt(jnp.mean(latent * latent, axis=1, keepdims=True) + epsilon)
    normed = latent * scale
    upstream = cotangent[...].astype(f32)
    scaled = upstream * gain[...]
    center = jnp.mean(scaled * normed, axis=1, keepdims=True)
    out[pl.ds(pl.multiple_of(step * 256, 256), 256), :] = (scale * (scaled - normed * center)).astype(bf16)
    gain_grad = jnp.sum(upstream * normed, axis=0, keepdims=True)

    @pl.when(step > 0)
    def _():
        out_gain = gain_grad + total_of(out)
        out[768:784, :] = split(out_gain)

    @pl.when(step == 0)
    def _():
        out[768:784, :] = split(gain_grad)

    @pl.when(step == 2)
    def _():
        copy.wait()


def parts(value):
    high = value.astype(bf16).astype(f32)
    middle = (value - high).astype(bf16).astype(f32)
    return [high, middle, value - high - middle]


def split(value):
    return jnp.concatenate(parts(value) + [jnp.zeros((13, 512), f32)], axis=0).astype(bf16)


def total_of(rows):
    return jnp.sum(rows[768:784, :].astype(f32), axis=0, keepdims=True)


def latent_grads(place, inputs, cotangent, gain, pieces):
    return pl.pallas_call(
        latent_kernel,
        grid_spec=pltpu.PrefetchScalarGridSpec(
            num_scalar_prefetch=1,
            grid=(3,),
            in_specs=[
                pl.BlockSpec((256, 7168), lambda i, place: (i, 0)),
                pl.BlockSpec((256, 512), lambda i, place: (i, 0)),
                pl.BlockSpec((1, 512), lambda i, place: (0, 0)),
            ]
            + [pl.BlockSpec(memory_space=pltpu.VMEM)] * 8,
            out_specs=[
                pl.BlockSpec((784, 512), lambda i, place: (0, 0)),
                pl.BlockSpec(memory_space=pl.ANY),
            ],
            scratch_shapes=[pltpu.VMEM((7168, 512), bf16), pltpu.SemaphoreType.DMA],
        ),
        out_shape=[jax.ShapeDtypeStruct((784, 512), bf16), jax.ShapeDtypeStruct((7168, 512), bf16)],
        compiler_params=pltpu.CompilerParams(vmem_limit_bytes=24 * MIB),
        cost_estimate=pl.CostEstimate(flops=2 * 768 * 7168 * 512, bytes_accessed=28 * MIB, transcendentals=768),
        name="latent",
    )(place, inputs, cotangent, gain, *pieces)


def input_kernel(grad, weight, before, out, token):
    token[...] = jnp.zeros((8, 128), f32)
    out[...] = lax.dot_general(
        grad[:768, :], weight[...], (((1,), (1,)), ((), ())), preferred_element_type=f32
    ).astype(bf16)


def input_grads(grad, weight, token):
    return pl.pallas_call(
        input_kernel,
        grid=(7,),
        in_specs=[
            pl.BlockSpec((784, 512), lambda i: (0, 0)),
            pl.BlockSpec((1024, 512), lambda i: (i, 0)),
            pl.BlockSpec((8, 128), lambda i: (0, 0)),
        ],
        out_specs=[pl.BlockSpec((768, 1024), lambda i: (0, i)), pl.BlockSpec((8, 128), lambda i: (0, 0))],
        out_shape=[jax.ShapeDtypeStruct((768, 7168), bf16), order],
        compiler_params=pltpu.CompilerParams(vmem_limit_bytes=52 * MIB),
        cost_estimate=pl.CostEstimate(flops=0, bytes_accessed=MIB, transcendentals=0),
        name="input_grads",
    )(grad, weight, token)


lanes = [slice(128 * i, 128 * i + 128) for i in four]


def flat(rows):
    return jnp.concatenate([rows[:, lane] for lane in lanes], axis=0)


def weight_kernel(place, *refs):
    mine, other, mine_grad, other_grad = refs[:2], refs[2:4], *refs[4:6]
    out, token, held = refs[-3:]
    token[...] = jnp.zeros((8, 128), f32)
    rows = jnp.concatenate([mine[0][...], mine[1][...]], axis=0)
    product = jnp.dot(rows, mine_grad[:768, :], preferred_element_type=f32)
    rows = jnp.concatenate([other[0][...], other[1][...]], axis=0)
    product += jnp.dot(rows, other_grad[:768, :], preferred_element_type=f32)
    held[...] = product.reshape(8, 56, 512)
    for i in range(8):
        out[0, 224 * i : 224 * i + 224, :] = flat(held[i]).astype(bf16)
    gain = total_of(mine_grad) + total_of(other_grad)
    out[0, 1792:1808, :] = gain_rows(flat(gain))


def gain_rows(gain):
    return jnp.concatenate(parts(gain) + [jnp.zeros((4, 128), f32)], axis=0).astype(bf16)


def gain_of(rows):
    rows = rows.astype(f32)
    return (rows[0:4] + rows[4:8]) + rows[8:12]


def weight_grads(place, mine, other, mine_grad, other_grad, by, tokens):
    def rows(i):
        def index(pair, place):
            x_ahead = lax.rem(place[0] + by, 4) * 4 + pair * 2 + i
            y_ahead = (pair * 2 + i) * 4 + lax.rem(place[2] + by, 4)
            return jnp.where(place[1] == 0, x_ahead, y_ahead), 0

        return pl.BlockSpec((224, 768), index)

    whole = pl.BlockSpec((784, 512), lambda pair, place: (0, 0))
    small = pl.BlockSpec((8, 128), lambda pair, place: (0, 0))
    return pl.pallas_call(
        weight_kernel,
        grid_spec=pltpu.PrefetchScalarGridSpec(
            num_scalar_prefetch=1,
            grid=(2,),
            in_specs=[rows(0), rows(1)] * 2 + [whole] * 2 + [small] * len(tokens),
            out_specs=[pl.BlockSpec((1, 1808, 128), lambda pair, place: (pair, 0, 0)), small],
            scratch_shapes=[pltpu.VMEM((8, 56, 512), f32)],
        ),
        out_shape=[jax.ShapeDtypeStruct((2, 1808, 128), bf16), order],
        compiler_params=pltpu.CompilerParams(vmem_limit_bytes=14 * MIB),
        cost_estimate=pl.CostEstimate(flops=0, bytes_accessed=MIB, transcendentals=0),
        name="weight_grads",
    )(place, mine, mine, other, other, mine_grad, other_grad, *tokens)


def add(values):
    own, one, two, three = [value.astype(f32) for value in values]
    return (own + two) + (one + three)


def first_kernel(place, *refs):
    partial, out = refs[:4], refs[-4:]
    other = jnp.where(place[1] == 0, place[2], place[0])
    for to in four:
        at = lax.rem(other + to, 4)
        for z in four:
            rows = pl.ds(pl.multiple_of(lax.rem(at, 2) * 896 + z * 224, 32), 224)
            out[to][224 * z : 224 * z + 224, :] = add([ref[lax.div(at, 2), rows, :] for ref in partial]).astype(bf16)
        for i in four:
            out[to][896 + 16 * i : 912 + 16 * i, :] = partial[i][0, 1792:1808, :]


def second_kernel(place, *refs):
    sums, out, held = refs[:4], refs[4:8], refs[8]
    x, core, y, z = [place[i] for i in four]
    for i in four:
        held[i] = sums[i][896:960, :].astype(f32)
    gain = jnp.zeros((4, 128), f32)
    for from_x in four:
        for from_y in four:
            back_x, back_y = lax.rem(x + 4 - from_x, 4), lax.rem(y + 4 - from_y, 4)
            major, other = jnp.where(core == 0, back_x, back_y), jnp.where(core == 0, back_y, back_x)
            gain = gain + gain_of(held[other, pl.ds(pl.multiple_of(major * 16, 16), 16), :])
    for to in four:
        rows = pl.ds(pl.multiple_of(lax.rem(z + to, 4) * 224, 32), 224)
        out[to][0:224, :] = add([ref[rows, :] for ref in sums]).astype(bf16)
        out[to][224:240, :] = gain_rows(gain)


def third_kernel(place, *refs):
    sums, weight_grad, gain_grad = refs[:4], *refs[4:]
    total = add([ref[0:224, :] for ref in sums])
    for i in four:
        weight_grad[:, lanes[i]] = total[56 * i : 56 * i + 56, :]
    gain_grad[...] = add([gain_of(ref[224:240, :]) for ref in sums])


def touch_kernel(value, token, out):
    out[...] = token[...] + value[0, 0:8, :].astype(f32)


def touch(value, token):
    return pl.pallas_call(
        touch_kernel,
        grid=(1,),
        in_specs=[pl.BlockSpec((1, 16, 128), lambda i: (0, 0, 0)), pl.BlockSpec((8, 128), lambda i: (0, 0))],
        out_specs=pl.BlockSpec((8, 128), lambda i: (0, 0)),
        out_shape=order,
        compiler_params=pltpu.CompilerParams(vmem_limit_bytes=4 * MIB),
        cost_estimate=pl.CostEstimate(flops=0, bytes_accessed=4096, transcendentals=0),
        name="touch",
    )(value, token)


def combine(kernel, shapes, place, values, scratch=(), tokens=()):
    vmem = pl.BlockSpec(memory_space=pltpu.VMEM)
    return pl.pallas_call(
        kernel,
        in_specs=[pl.BlockSpec(memory_space=pltpu.SMEM)]
        + [vmem] * (len(values) + len(tokens)),
        out_specs=[vmem] * len(shapes),
        out_shape=[jax.ShapeDtypeStruct(*shape) for shape in shapes],
        scratch_shapes=list(scratch),
        compiler_params=pltpu.CompilerParams(vmem_limit_bytes=24 * MIB),
        cost_estimate=pl.CostEstimate(flops=0, bytes_accessed=MIB, transcendentals=0),
        name=kernel.__name__,
    )(place, *values, *tokens)


def along_major(value, by):
    return fetch(value, lambda x, c, y, z: (x, c, y - by, z) if c else (x - by, c, y, z))


def along_other(value, by):
    return fetch(value, lambda x, c, y, z: (x - by, c, y, z) if c else (x, c, y - by, z))


def along_z(value, by):
    return fetch(value, lambda x, c, y, z: (x, c, y, z - by))


def exchange(values, along):
    return [values[0]] + [along(values[by], by) for by in (1, 2, 3)]


def reduce_scatter(place, partial, token):
    sums = exchange(partial, along_major)
    token = touch(sums[1], touch(sums[2], token))
    sums = combine(first_kernel, [((960, 128), bf16)] * 4, place, sums, tokens=[token])
    sums = exchange(sums, along_other)
    sums = combine(second_kernel, [((240, 128), bf16)] * 4, place, sums, [pltpu.VMEM((4, 64, 128), f32)])
    sums = exchange(sums, along_z)
    return combine(third_kernel, [((56, 512), f32), ((4, 128), f32)], place, sums)


def shards(inputs, cotangent, weight, norm_gain):
    dp, shard = lax.axis_index("dp"), lax.axis_index("shard")
    core = dp % 2
    place = jnp.stack([dp // 2, core, shard // 4, shard % 4]).astype(jnp.int32)
    half = lax.dynamic_slice_in_dim(weight, core * 224, 224, 0)
    other_inputs = twin(inputs)
    kept, token = turn(place, inputs)
    line = join([half] + [fetch_first(half, by) for by in (1, 2, 3)], token)
    mine = [line] + [fetch_second(line, by) for by in (1, 2, 3)]
    other, token = turn(place, other_inputs)
    mine[3] = tie(mine[3], token)
    pieces = mine + [twin(piece) for piece in mine]
    latent_grad, gathered = latent_grads(place, inputs, cotangent, norm_gain.reshape(1, 512), pieces)
    other_grad = twin(latent_grad)
    partial, tokens = [None] * 4, []
    for by in (2, 1, 3, 0):
        partial[by], token = weight_grads(place, kept, other, latent_grad, other_grad, by, tokens)
        tokens = [token]
    input_grad, token = input_grads(latent_grad, gathered, token)
    weight_grad, gain_grad = reduce_scatter(place, partial, token)
    return (input_grad, weight_grad, gain_grad.reshape(512))


def solution(mesh):
    placed = (P(("dp", "shard"), None), P(("dp", "shard"), None), P("shard", None), P())
    return jax.shard_map(
        shards,
        mesh=mesh,
        in_specs=placed,
        out_specs=(P(("dp", "shard"), None), P(("dp", "shard"), None), P()),
        check_vma=False,
    )
```

```python
import functools

import jax
import jax.numpy as jnp
from jax import lax
from jax.experimental import pallas as pl
from jax.experimental.pallas import tpu as pltpu
from jax.sharding import PartitionSpec as P

epsilon = 1e-06
axes = ("dp", "shard")
bf16, f32 = jnp.bfloat16, jnp.float32
MIB = 1024 * 1024


def device(x, core, y, z):
    return ((x % 4) * 2 + core) * 16 + (y % 4) * 4 + z % 4


four = range(4)
spots = [(x, c, y, z) for x in four for c in range(2) for y in four for z in four]


def fetch(value, source):
    return lax.ppermute(value, axes, [(device(*source(*spot)), device(*spot)) for spot in spots])


def twin(value):
    return fetch(value, lambda x, c, y, z: (x, 1 - c, y, z))


def fetch_first(value, by):
    return fetch(value, lambda x, c, y, z: (x, c, y, z + by) if c else (x, c, y + by, z))


def fetch_second(value, by):
    return fetch(value, lambda x, c, y, z: (x, c, y + by, z) if c else (x, c, y, z + by))


order = jax.ShapeDtypeStruct((8, 128), f32)


def turn_kernel(place, rows, out, token):
    token[...] = jnp.zeros((8, 128), f32)
    for column in range(0, 896, 128):
        out[column : column + 128, :] = rows[:, column : column + 128].T


def turn(place, inputs):
    return pl.pallas_call(
        turn_kernel,
        grid_spec=pltpu.PrefetchScalarGridSpec(
            num_scalar_prefetch=1,
            grid=(4,),
            in_specs=[pl.BlockSpec((768, 896), lambda i, place: (0, 2 * i + place[1]))],
            out_specs=[
                pl.BlockSpec((896, 768), lambda i, place: (i, 0)),
                pl.BlockSpec((8, 128), lambda i, place: (0, 0)),
            ],
        ),
        out_shape=[jax.ShapeDtypeStruct((3584, 768), bf16), order],
        compiler_params=pltpu.CompilerParams(vmem_limit_bytes=16 * MIB),
        cost_estimate=pl.CostEstimate(flops=0, bytes_accessed=22 * MIB, transcendentals=0),
        name="turn",
    )(place, inputs)


def tie_kernel(value, *refs):
    refs[-1][...] = value[...]


def tie(value, *tokens):
    vmem = pl.BlockSpec(memory_space=pltpu.VMEM)
    return pl.pallas_call(
        tie_kernel,
        in_specs=[vmem] * (1 + len(tokens)),
        out_specs=vmem,
        out_shape=jax.ShapeDtypeStruct(value.shape, value.dtype),
        compiler_params=pltpu.CompilerParams(vmem_limit_bytes=8 * MIB),
        cost_estimate=pl.CostEstimate(flops=0, bytes_accessed=2 * MIB, transcendentals=0),
        name="tie",
    )(value, *tokens)


def join_kernel(one, two, three, four_, token, out):
    for i, ref in enumerate((one, two, three, four_)):
        out[i] = ref[...]


def join(values, token):
    vmem = pl.BlockSpec(memory_space=pltpu.VMEM)
    return pl.pallas_call(
        join_kernel,
        in_specs=[vmem] * 5,
        out_specs=vmem,
        out_shape=jax.ShapeDtypeStruct((4, 448, 256), bf16),
        compiler_params=pltpu.CompilerParams(vmem_limit_bytes=8 * MIB),
        cost_estimate=pl.CostEstimate(flops=0, bytes_accessed=2 * MIB, transcendentals=0),
        name="join",
    )(*values, token)


def spot(place, side, far, near):
    part = place[1] if side == 0 else 1 - place[1]
    along_y = lax.rem(place[2] + jnp.where(part == 0, near, far), 4)
    along_z = lax.rem(place[3] + jnp.where(part == 0, far, near), 4)
    return along_y * 4 + along_z, part


def norm(place, first, second, cotangent, gain, out, row):
    core = place[1]
    own = pl.ds(pl.multiple_of(core * 256, 256), 256)
    other = pl.ds(pl.multiple_of(256 - core * 256, 256), 256)

    def body(i, sums):
        tokens = pl.ds(pl.multiple_of(i * 64, 64), 64)
        latent = [first[tokens, :], second[tokens, :]]
        square = sum(jnp.sum(value * value, axis=1, keepdims=True) for value in latent)
        scale = lax.rsqrt(square * (1.0 / 512) + epsilon)
        normed = [value * scale for value in latent]
        upstream = [cotangent[tokens, lane].astype(f32) for lane in (own, other)]
        scaled = [value * gain[:, lane] for value, lane in zip(upstream, (own, other))]
        center = sum(jnp.sum(u * v, axis=1, keepdims=True) for u, v in zip(scaled, normed)) * (1.0 / 512)
        for lane, u, v in zip((own, other), scaled, normed):
            out[tokens, lane] = (scale * (u - v * center)).astype(bf16)
        return tuple(
            total + jnp.sum((u * v).reshape(8, 8, 256), axis=0) for total, u, v in zip(sums, upstream, normed)
        )

    sums = lax.fori_loop(0, 12, body, (jnp.zeros((8, 256), f32),) * 2, unroll=2)
    for lane, value in zip((own, other), sums):
        row[:, lane] = jnp.broadcast_to(jnp.sum(value, axis=0, keepdims=True), (8, 256))
    out[768:784, :] = split(row[0:1, :])


def latent_kernel(side, far, has_before, last, place, inputs, piece, *refs):
    at = 1 * has_before
    ending = refs[at : at + 3 * last]
    out, token, filled, window, arrive, *extra = refs[at + 3 * last :]
    token[...] = jnp.zeros((8, 128), f32)
    total = extra[0] if last else out
    copies = []
    for near in four:
        block, part = spot(place, side, far, near)
        first = pl.multiple_of(lax.div(block * 7, 2) * 128, 128)
        copy = pltpu.make_async_copy(
            inputs.at[:, pl.ds(first, 512)], window.at[:, 512 * near : 512 * near + 512], arrive.at[near]
        )
        copy.start()
        copies.append(copy)
    for near in four:
        block, part = spot(place, side, far, near)
        odd = lax.rem(block, 2)
        filled[pl.ds(pl.multiple_of(512 * near + odd * 64, 64), 448), :] = piece[near]
        filled[pl.ds(pl.multiple_of(512 * near + 448 - odd * 448, 64), 64), :] = jnp.zeros((64, 256), bf16)
    for copy in copies:
        copy.wait()
    for start in range(0, 768, 256):
        product = jnp.dot(window[start : start + 256, :], filled[...], preferred_element_type=f32)
        total[start : start + 256, :] = refs[0][start : start + 256, :] + product if has_before else product
    if last:
        norm(place, ending[0], total, ending[1], ending[2], out, extra[1])


def latent_part(place, inputs, piece, side, far, before=None, ending=()):
    hbm, vmem = pl.BlockSpec(memory_space=pltpu.HBM), pl.BlockSpec(memory_space=pltpu.VMEM)
    last = len(ending) > 0
    operands = [place, inputs, piece] + ([] if before is None else [before]) + list(ending)
    specs = [pl.BlockSpec(memory_space=pltpu.SMEM), hbm] + [vmem] * (len(operands) - 2)
    scratch = [pltpu.VMEM((2048, 256), bf16), pltpu.VMEM((768, 2048), bf16), pltpu.SemaphoreType.DMA((4,))]
    out = jax.ShapeDtypeStruct((768, 256), f32)
    if last:
        scratch += [pltpu.VMEM((768, 256), f32), pltpu.VMEM((8, 512), f32)]
        out = jax.ShapeDtypeStruct((784, 512), bf16)
    return pl.pallas_call(
        functools.partial(latent_kernel, side, far, before is not None, last),
        in_specs=specs,
        out_specs=[vmem] * 2,
        scratch_shapes=scratch,
        out_shape=[out, order],
        compiler_params=pltpu.CompilerParams(vmem_limit_bytes=14 * MIB),
        cost_estimate=pl.CostEstimate(flops=768 * 2048 * 512, bytes_accessed=6 * MIB, transcendentals=0),
        name="latent",
    )(*operands)


def assemble_kernel(place, *refs):
    out = refs[9]
    for side in range(2):
        for far in four:
            for near in four:
                block, part = spot(place, side, far, near)
                rows = pl.ds(pl.multiple_of(block * 448, 64), 448)
                columns = pl.ds(pl.multiple_of(part * 256, 256), 256)
                out[rows, columns] = refs[side * 4 + far][near]


def assemble(place, pieces, token):
    vmem = pl.BlockSpec(memory_space=pltpu.VMEM)
    return pl.pallas_call(
        assemble_kernel,
        in_specs=[pl.BlockSpec(memory_space=pltpu.SMEM)] + [vmem] * 9,
        out_specs=vmem,
        out_shape=jax.ShapeDtypeStruct((7168, 512), bf16),
        compiler_params=pltpu.CompilerParams(vmem_limit_bytes=20 * MIB),
        cost_estimate=pl.CostEstimate(flops=0, bytes_accessed=MIB, transcendentals=0),
        name="assemble",
    )(place, *pieces, token)


def parts(value):
    high = value.astype(bf16).astype(f32)
    middle = (value - high).astype(bf16).astype(f32)
    return [high, middle, value - high - middle]


def split(value):
    return jnp.concatenate(parts(value) + [jnp.zeros((13, 512), f32)], axis=0).astype(bf16)


def total_of(rows):
    return jnp.sum(rows[768:784, :].astype(f32), axis=0, keepdims=True)


def input_kernel(grad, weight, before, *refs):
    out, token = refs[-2:]
    token[...] = jnp.zeros((8, 128), f32)
    out[...] = lax.dot_general(
        grad[:768, :], weight[...], (((1,), (1,)), ((), ())), preferred_element_type=f32
    ).astype(bf16)


def input_grads(grad, weight, token, first, count, begun=()):
    small = pl.BlockSpec((8, 128), lambda i: (0, 0))
    return pl.pallas_call(
        input_kernel,
        grid=(count,),
        in_specs=[
            pl.BlockSpec((784, 512), lambda i: (0, 0)),
            pl.BlockSpec((1024, 512), lambda i: (first + i, 0)),
            small,
        ]
        + [pl.BlockSpec(memory_space=pltpu.HBM)] * len(begun),
        out_specs=[pl.BlockSpec((768, 1024), lambda i: (0, first + i)), small],
        out_shape=[jax.ShapeDtypeStruct((768, 7168), bf16), order],
        input_output_aliases={3: 0} if begun else {},
        compiler_params=pltpu.CompilerParams(vmem_limit_bytes=40 * MIB),
        cost_estimate=pl.CostEstimate(flops=0, bytes_accessed=MIB, transcendentals=0),
        name="input_grads",
    )(grad, weight, token, *begun)


lanes = [slice(128 * i, 128 * i + 128) for i in four]


def flat(rows):
    return jnp.concatenate([rows[:, lane] for lane in lanes], axis=0)


def weight_kernel(place, *refs):
    mine, other, mine_grad, other_grad = refs[:2], refs[2:4], *refs[4:6]
    out, token, held = refs[-3:]
    token[...] = jnp.zeros((8, 128), f32)
    rows = jnp.concatenate([mine[0][...], mine[1][...]], axis=0)
    product = jnp.dot(rows, mine_grad[:768, :], preferred_element_type=f32)
    rows = jnp.concatenate([other[0][...], other[1][...]], axis=0)
    product += jnp.dot(rows, other_grad[:768, :], preferred_element_type=f32)
    held[...] = product.reshape(8, 56, 512)
    for i in range(8):
        out[0, 224 * i : 224 * i + 224, :] = flat(held[i]).astype(bf16)
    gain = total_of(mine_grad) + total_of(other_grad)
    out[0, 1792:1808, :] = gain_rows(flat(gain))


def gain_rows(gain):
    return jnp.concatenate(parts(gain) + [jnp.zeros((4, 128), f32)], axis=0).astype(bf16)


def gain_of(rows):
    rows = rows.astype(f32)
    return (rows[0:4] + rows[4:8]) + rows[8:12]


def weight_grads(place, mine, other, mine_grad, other_grad, by, tokens):
    def rows(i):
        def index(pair, place):
            x_ahead = lax.rem(place[0] + by, 4) * 4 + pair * 2 + i
            y_ahead = (pair * 2 + i) * 4 + lax.rem(place[2] + by, 4)
            return jnp.where(place[1] == 0, x_ahead, y_ahead), 0

        return pl.BlockSpec((224, 768), index)

    whole = pl.BlockSpec((784, 512), lambda pair, place: (0, 0))
    small = pl.BlockSpec((8, 128), lambda pair, place: (0, 0))
    return pl.pallas_call(
        weight_kernel,
        grid_spec=pltpu.PrefetchScalarGridSpec(
            num_scalar_prefetch=1,
            grid=(2,),
            in_specs=[rows(0), rows(1)] * 2 + [whole] * 2 + [small] * len(tokens),
            out_specs=[pl.BlockSpec((1, 1808, 128), lambda pair, place: (pair, 0, 0)), small],
            scratch_shapes=[pltpu.VMEM((8, 56, 512), f32)],
        ),
        out_shape=[jax.ShapeDtypeStruct((2, 1808, 128), bf16), order],
        compiler_params=pltpu.CompilerParams(vmem_limit_bytes=14 * MIB),
        cost_estimate=pl.CostEstimate(flops=0, bytes_accessed=MIB, transcendentals=0),
        name="weight_grads",
    )(place, mine, mine, other, other, mine_grad, other_grad, *tokens)


def add(values):
    own, one, two, three = [value.astype(f32) for value in values]
    return (own + two) + (one + three)


def first_kernel(place, *refs):
    partial, out, token = refs[:4], refs[-5:-1], refs[-1]
    token[...] = jnp.zeros((8, 128), f32)
    other = jnp.where(place[1] == 0, place[2], place[0])
    for to in four:
        at = lax.rem(other + to, 4)
        for z in four:
            rows = pl.ds(pl.multiple_of(lax.rem(at, 2) * 896 + z * 224, 32), 224)
            out[to][224 * z : 224 * z + 224, :] = add([ref[lax.div(at, 2), rows, :] for ref in partial]).astype(bf16)
        for i in four:
            out[to][896 + 16 * i : 912 + 16 * i, :] = partial[i][0, 1792:1808, :]


def second_kernel(place, *refs):
    sums, out, held = refs[:4], refs[5:9], refs[9]
    x, core, y, z = [place[i] for i in four]
    for i in four:
        held[i] = sums[i][896:960, :].astype(f32)
    gain = jnp.zeros((4, 128), f32)
    for from_x in four:
        for from_y in four:
            back_x, back_y = lax.rem(x + 4 - from_x, 4), lax.rem(y + 4 - from_y, 4)
            major, other = jnp.where(core == 0, back_x, back_y), jnp.where(core == 0, back_y, back_x)
            gain = gain + gain_of(held[other, pl.ds(pl.multiple_of(major * 16, 16), 16), :])
    for to in four:
        rows = pl.ds(pl.multiple_of(lax.rem(z + to, 4) * 224, 32), 224)
        out[to][0:224, :] = add([ref[rows, :] for ref in sums]).astype(bf16)
        out[to][224:240, :] = gain_rows(gain)


def third_kernel(place, *refs):
    sums, weight_grad, gain_grad = refs[:4], *refs[4:]
    total = add([ref[0:224, :] for ref in sums])
    for i in four:
        weight_grad[:, lanes[i]] = total[56 * i : 56 * i + 56, :]
    gain_grad[...] = add([gain_of(ref[224:240, :]) for ref in sums])


def touch_kernel(value, token, out):
    out[...] = token[...] + value[0, 0:8, :].astype(f32)


def touch(value, token):
    return pl.pallas_call(
        touch_kernel,
        grid=(1,),
        in_specs=[pl.BlockSpec((1, 16, 128), lambda i: (0, 0, 0)), pl.BlockSpec((8, 128), lambda i: (0, 0))],
        out_specs=pl.BlockSpec((8, 128), lambda i: (0, 0)),
        out_shape=order,
        compiler_params=pltpu.CompilerParams(vmem_limit_bytes=4 * MIB),
        cost_estimate=pl.CostEstimate(flops=0, bytes_accessed=4096, transcendentals=0),
        name="touch",
    )(value, token)


def combine(kernel, shapes, place, values, scratch=(), tokens=()):
    vmem = pl.BlockSpec(memory_space=pltpu.VMEM)
    return pl.pallas_call(
        kernel,
        in_specs=[pl.BlockSpec(memory_space=pltpu.SMEM)]
        + [vmem] * (len(values) + len(tokens)),
        out_specs=[vmem] * len(shapes),
        out_shape=[jax.ShapeDtypeStruct(*shape) for shape in shapes],
        scratch_shapes=list(scratch),
        compiler_params=pltpu.CompilerParams(vmem_limit_bytes=24 * MIB),
        cost_estimate=pl.CostEstimate(flops=0, bytes_accessed=MIB, transcendentals=0),
        name=kernel.__name__,
    )(place, *values, *tokens)


def along_major(value, by):
    return fetch(value, lambda x, c, y, z: (x, c, y - by, z) if c else (x - by, c, y, z))


def along_other(value, by):
    return fetch(value, lambda x, c, y, z: (x - by, c, y, z) if c else (x, c, y - by, z))


def along_z(value, by):
    return fetch(value, lambda x, c, y, z: (x, c, y, z - by))


def exchange(values, along):
    return [values[0]] + [along(values[by], by) for by in (1, 2, 3)]


def first_sums(place, partial, latent_grad, gathered, token):
    sums = exchange(partial, along_major)
    input_grad, token = input_grads(latent_grad, gathered, token, 0, 4)
    token = touch(sums[1], touch(sums[2], token))
    outs = [((960, 128), bf16)] * 4 + [((8, 128), f32)]
    return combine(first_kernel, outs, place, sums, tokens=[token]), input_grad


def last_sums(place, sums, latent_grad, gathered, input_grad):
    token = sums[4]
    sums = exchange(sums[:4], along_other)
    input_grad, token = input_grads(latent_grad, gathered, token, 4, 3, [input_grad])
    scratch = [pltpu.VMEM((4, 64, 128), f32)]
    sums = combine(second_kernel, [((240, 128), bf16)] * 4, place, sums, scratch, [token])
    sums = exchange(sums, along_z)
    return *combine(third_kernel, [((56, 512), f32), ((4, 128), f32)], place, sums), input_grad


def shards(inputs, cotangent, weight, norm_gain):
    dp, shard = lax.axis_index("dp"), lax.axis_index("shard")
    core = dp % 2
    place = jnp.stack([dp // 2, core, shard // 4, shard % 4]).astype(jnp.int32)
    half = lax.dynamic_slice_in_dim(weight, core * 256, 256, 1)
    other_inputs = twin(inputs)
    kept, token = turn(place, inputs)
    line = join([half] + [fetch_first(half, by) for by in (1, 2, 3)], token)
    mine = [line] + [fetch_second(line, by) for by in (1, 2, 3)]
    other, token = turn(place, other_inputs)
    gain = norm_gain.reshape(1, 512)
    parts_of = functools.partial(latent_part, place, inputs)
    theirs = [twin(line)]
    first, _ = parts_of(mine[0], 0, 0)
    second, done = parts_of(theirs[0], 1, 0)
    mine[1] = tie(mine[1], token, done)
    theirs.append(twin(mine[1]))
    theirs.append(twin(mine[2]))
    first, _ = parts_of(mine[1], 0, 1, first)
    first, done = parts_of(mine[2], 0, 2, first)
    second, after = parts_of(theirs[1], 1, 1, second)
    mine[3] = tie(mine[3], done, after)
    theirs.append(twin(mine[3]))
    second, _ = parts_of(theirs[2], 1, 2, second)
    first, _ = parts_of(mine[3], 0, 3, first)
    second, _ = parts_of(theirs[3], 1, 3, second, (first, cotangent, gain))
    latent_grad = second
    other_grad = twin(latent_grad)
    partial, tokens = [None] * 4, []
    for by in (2, 1, 3, 0):
        partial[by], token = weight_grads(place, kept, other, latent_grad, other_grad, by, tokens)
        tokens = [token]
    gathered = assemble(place, mine + theirs, token)
    sums, input_grad = first_sums(place, partial, latent_grad, gathered, token)
    weight_grad, gain_grad, input_grad = last_sums(place, sums, latent_grad, gathered, input_grad)
    return (input_grad, weight_grad, gain_grad.reshape(512))


def solution(mesh):
    placed = (P(("dp", "shard"), None), P(("dp", "shard"), None), P("shard", None), P())
    return jax.shard_map(
        shards,
        mesh=mesh,
        in_specs=placed,
        out_specs=(P(("dp", "shard"), None), P(("dp", "shard"), None), P()),
        check_vma=False,
    )
```

```python
import functools

import jax
import jax.numpy as jnp
from jax import lax
from jax.experimental import pallas as pl
from jax.experimental.pallas import tpu as pltpu
from jax.sharding import PartitionSpec as P

epsilon = 1e-06
axes = ("dp", "shard")
bf16, f32 = jnp.bfloat16, jnp.float32
MIB = 1024 * 1024


def device(x, core, y, z):
    return ((x % 4) * 2 + core) * 16 + (y % 4) * 4 + z % 4


four = range(4)
spots = [(x, c, y, z) for x in four for c in range(2) for y in four for z in four]


def fetch(value, source):
    return lax.ppermute(value, axes, [(device(*source(*spot)), device(*spot)) for spot in spots])


def twin(value):
    return fetch(value, lambda x, c, y, z: (x, 1 - c, y, z))


def fetch_first(value, by):
    return fetch(value, lambda x, c, y, z: (x, c, y, z + by) if c else (x, c, y + by, z))


def fetch_second(value, by):
    return fetch(value, lambda x, c, y, z: (x, c, y + by, z) if c else (x, c, y, z + by))


order = jax.ShapeDtypeStruct((8, 128), f32)


def turn_kernel(place, rows, out, token):
    token[...] = jnp.zeros((8, 128), f32)
    for column in range(0, 896, 128):
        out[column : column + 128, :] = rows[:, column : column + 128].T


def turn(place, inputs):
    return pl.pallas_call(
        turn_kernel,
        grid_spec=pltpu.PrefetchScalarGridSpec(
            num_scalar_prefetch=1,
            grid=(4,),
            in_specs=[pl.BlockSpec((768, 896), lambda i, place: (0, 2 * i + place[1]))],
            out_specs=[
                pl.BlockSpec((896, 768), lambda i, place: (i, 0)),
                pl.BlockSpec((8, 128), lambda i, place: (0, 0)),
            ],
        ),
        out_shape=[jax.ShapeDtypeStruct((3584, 768), bf16), order],
        compiler_params=pltpu.CompilerParams(vmem_limit_bytes=16 * MIB),
        cost_estimate=pl.CostEstimate(flops=0, bytes_accessed=22 * MIB, transcendentals=0),
        name="turn",
    )(place, inputs)


def tie_kernel(value, *refs):
    refs[-1][...] = value[...]


def tie(value, *tokens):
    vmem = pl.BlockSpec(memory_space=pltpu.VMEM)
    return pl.pallas_call(
        tie_kernel,
        in_specs=[vmem] * (1 + len(tokens)),
        out_specs=vmem,
        out_shape=jax.ShapeDtypeStruct(value.shape, value.dtype),
        compiler_params=pltpu.CompilerParams(vmem_limit_bytes=8 * MIB),
        cost_estimate=pl.CostEstimate(flops=0, bytes_accessed=4096, transcendentals=0),
        name="tie",
    )(value, *tokens)


def join_kernel(one, two, three, four_, token, out):
    for i, ref in enumerate((one, two, three, four_)):
        out[i] = ref[...]


def join(values, token):
    vmem = pl.BlockSpec(memory_space=pltpu.VMEM)
    return pl.pallas_call(
        join_kernel,
        in_specs=[vmem] * 5,
        out_specs=vmem,
        out_shape=jax.ShapeDtypeStruct((4, 448, 256), bf16),
        compiler_params=pltpu.CompilerParams(vmem_limit_bytes=8 * MIB),
        cost_estimate=pl.CostEstimate(flops=0, bytes_accessed=2 * MIB, transcendentals=0),
        name="join",
    )(*values, token)


def spot(place, side, far, near):
    part = place[1] if side == 0 else 1 - place[1]
    along_y = lax.rem(place[2] + jnp.where(part == 0, near, far), 4)
    along_z = lax.rem(place[3] + jnp.where(part == 0, far, near), 4)
    return along_y * 4 + along_z, part


def norm(place, first, second, cotangent, gain, out, row):
    core = place[1]
    own = pl.ds(pl.multiple_of(core * 256, 256), 256)
    other = pl.ds(pl.multiple_of(256 - core * 256, 256), 256)

    def body(i, sums):
        tokens = pl.ds(pl.multiple_of(i * 64, 64), 64)
        latent = [first[tokens, :], second[tokens, :]]
        square = sum(jnp.sum(value * value, axis=1, keepdims=True) for value in latent)
        scale = lax.rsqrt(square * (1.0 / 512) + epsilon)
        normed = [value * scale for value in latent]
        upstream = [cotangent[tokens, lane].astype(f32) for lane in (own, other)]
        scaled = [value * gain[:, lane] for value, lane in zip(upstream, (own, other))]
        center = sum(jnp.sum(u * v, axis=1, keepdims=True) for u, v in zip(scaled, normed)) * (1.0 / 512)
        for lane, u, v in zip((own, other), scaled, normed):
            out[tokens, lane] = (scale * (u - v * center)).astype(bf16)
        return tuple(
            total + jnp.sum((u * v).reshape(8, 8, 256), axis=0) for total, u, v in zip(sums, upstream, normed)
        )

    sums = lax.fori_loop(0, 12, body, (jnp.zeros((8, 256), f32),) * 2, unroll=2)
    for lane, value in zip((own, other), sums):
        row[:, lane] = jnp.broadcast_to(jnp.sum(value, axis=0, keepdims=True), (8, 256))
    out[768:784, :] = split(row[0:1, :])


def latent_kernel(side, far, has_before, last, place, inputs, piece, *refs):
    at = 1 * has_before
    ending = refs[at : at + 3 * last]
    out, token, filled, window, arrive, *extra = refs[at + 3 * last :]
    token[...] = jnp.zeros((8, 128), f32)
    total = extra[0] if last else out
    copies = []
    for near in four:
        block, part = spot(place, side, far, near)
        first = pl.multiple_of(lax.div(block * 7, 2) * 128, 128)
        copy = pltpu.make_async_copy(
            inputs.at[:, pl.ds(first, 512)], window.at[:, 512 * near : 512 * near + 512], arrive.at[near]
        )
        copy.start()
        copies.append(copy)
    for near in four:
        block, part = spot(place, side, far, near)
        odd = lax.rem(block, 2)
        filled[pl.ds(pl.multiple_of(512 * near + odd * 64, 64), 448), :] = piece[near]
        filled[pl.ds(pl.multiple_of(512 * near + 448 - odd * 448, 64), 64), :] = jnp.zeros((64, 256), bf16)
    for copy in copies:
        copy.wait()
    for start in range(0, 768, 256):
        product = jnp.dot(window[start : start + 256, :], filled[...], preferred_element_type=f32)
        total[start : start + 256, :] = refs[0][start : start + 256, :] + product if has_before else product
    if last:
        norm(place, ending[0], total, ending[1], ending[2], out, extra[1])


def latent_part(place, inputs, piece, side, far, before=None, ending=()):
    hbm, vmem = pl.BlockSpec(memory_space=pltpu.HBM), pl.BlockSpec(memory_space=pltpu.VMEM)
    last = len(ending) > 0
    operands = [place, inputs, piece] + ([] if before is None else [before]) + list(ending)
    specs = [pl.BlockSpec(memory_space=pltpu.SMEM), hbm] + [vmem] * (len(operands) - 2)
    scratch = [pltpu.VMEM((2048, 256), bf16), pltpu.VMEM((768, 2048), bf16), pltpu.SemaphoreType.DMA((4,))]
    out = jax.ShapeDtypeStruct((768, 256), f32)
    if last:
        scratch += [pltpu.VMEM((768, 256), f32), pltpu.VMEM((8, 512), f32)]
        out = jax.ShapeDtypeStruct((784, 512), bf16)
    return pl.pallas_call(
        functools.partial(latent_kernel, side, far, before is not None, last),
        in_specs=specs,
        out_specs=[vmem] * 2,
        scratch_shapes=scratch,
        out_shape=[out, order],
        compiler_params=pltpu.CompilerParams(vmem_limit_bytes=14 * MIB),
        cost_estimate=pl.CostEstimate(flops=0, bytes_accessed=4096, transcendentals=0),
        name="latent",
    )(*operands)


def assemble_kernel(place, *refs):
    out = refs[9]
    for side in range(2):
        for far in four:
            for near in four:
                block, part = spot(place, side, far, near)
                rows = pl.ds(pl.multiple_of(block * 448, 64), 448)
                columns = pl.ds(pl.multiple_of(part * 256, 256), 256)
                out[rows, columns] = refs[side * 4 + far][near]


def assemble(place, pieces, token):
    vmem = pl.BlockSpec(memory_space=pltpu.VMEM)
    return pl.pallas_call(
        assemble_kernel,
        in_specs=[pl.BlockSpec(memory_space=pltpu.SMEM)] + [vmem] * 9,
        out_specs=vmem,
        out_shape=jax.ShapeDtypeStruct((7168, 512), bf16),
        compiler_params=pltpu.CompilerParams(vmem_limit_bytes=20 * MIB),
        cost_estimate=pl.CostEstimate(flops=0, bytes_accessed=MIB, transcendentals=0),
        name="assemble",
    )(place, *pieces, token)


def parts(value):
    high = value.astype(bf16).astype(f32)
    middle = (value - high).astype(bf16).astype(f32)
    return [high, middle, value - high - middle]


def split(value):
    return jnp.concatenate(parts(value) + [jnp.zeros((13, 512), f32)], axis=0).astype(bf16)


def total_of(rows):
    return jnp.sum(rows[768:784, :].astype(f32), axis=0, keepdims=True)


def input_kernel(grad, weight, before, *refs):
    out, token = refs[-2:]
    token[...] = jnp.zeros((8, 128), f32)
    out[...] = lax.dot_general(
        grad[:768, :], weight[...], (((1,), (1,)), ((), ())), preferred_element_type=f32
    ).astype(bf16)


def input_grads(grad, weight, token, first, count, begun=()):
    small = pl.BlockSpec((8, 128), lambda i: (0, 0))
    return pl.pallas_call(
        input_kernel,
        grid=(count,),
        in_specs=[
            pl.BlockSpec((784, 512), lambda i: (0, 0)),
            pl.BlockSpec((1024, 512), lambda i: (first + i, 0)),
            small,
        ]
        + [pl.BlockSpec(memory_space=pltpu.HBM)] * len(begun),
        out_specs=[pl.BlockSpec((768, 1024), lambda i: (0, first + i)), small],
        out_shape=[jax.ShapeDtypeStruct((768, 7168), bf16), order],
        input_output_aliases={3: 0} if begun else {},
        compiler_params=pltpu.CompilerParams(vmem_limit_bytes=40 * MIB),
        cost_estimate=pl.CostEstimate(flops=0, bytes_accessed=MIB, transcendentals=0),
        name="input_grads",
    )(grad, weight, token, *begun)


lanes = [slice(128 * i, 128 * i + 128) for i in four]


def flat(rows):
    return jnp.concatenate([rows[:, lane] for lane in lanes], axis=0)


def weight_kernel(place, *refs):
    mine, other, mine_grad, other_grad = refs[:2], refs[2:4], *refs[4:6]
    out, token, held = refs[-3:]
    token[...] = jnp.zeros((8, 128), f32)
    rows = jnp.concatenate([mine[0][...], mine[1][...]], axis=0)
    product = jnp.dot(rows, mine_grad[:768, :], preferred_element_type=f32)
    rows = jnp.concatenate([other[0][...], other[1][...]], axis=0)
    product += jnp.dot(rows, other_grad[:768, :], preferred_element_type=f32)
    held[...] = product.reshape(8, 56, 512)
    for i in range(8):
        out[0, 224 * i : 224 * i + 224, :] = flat(held[i]).astype(bf16)
    gain = total_of(mine_grad) + total_of(other_grad)
    out[0, 1792:1808, :] = gain_rows(flat(gain))


def gain_rows(gain):
    return jnp.concatenate(parts(gain) + [jnp.zeros((4, 128), f32)], axis=0).astype(bf16)


def gain_of(rows):
    rows = rows.astype(f32)
    return (rows[0:4] + rows[4:8]) + rows[8:12]


def weight_grads(place, mine, other, mine_grad, other_grad, by, tokens):
    def rows(i):
        def index(pair, place):
            x_ahead = lax.rem(place[0] + by, 4) * 4 + pair * 2 + i
            y_ahead = (pair * 2 + i) * 4 + lax.rem(place[2] + by, 4)
            return jnp.where(place[1] == 0, x_ahead, y_ahead), 0

        return pl.BlockSpec((224, 768), index)

    whole = pl.BlockSpec((784, 512), lambda pair, place: (0, 0))
    small = pl.BlockSpec((8, 128), lambda pair, place: (0, 0))
    return pl.pallas_call(
        weight_kernel,
        grid_spec=pltpu.PrefetchScalarGridSpec(
            num_scalar_prefetch=1,
            grid=(2,),
            in_specs=[rows(0), rows(1)] * 2 + [whole] * 2 + [small] * len(tokens),
            out_specs=[pl.BlockSpec((1, 1808, 128), lambda pair, place: (pair, 0, 0)), small],
            scratch_shapes=[pltpu.VMEM((8, 56, 512), f32)],
        ),
        out_shape=[jax.ShapeDtypeStruct((2, 1808, 128), bf16), order],
        compiler_params=pltpu.CompilerParams(vmem_limit_bytes=14 * MIB),
        cost_estimate=pl.CostEstimate(flops=0, bytes_accessed=MIB, transcendentals=0),
        name="weight_grads",
    )(place, mine, mine, other, other, mine_grad, other_grad, *tokens)


def add(values):
    own, one, two, three = [value.astype(f32) for value in values]
    return (own + two) + (one + three)


def first_kernel(place, *refs):
    partial, out, token = refs[:4], refs[-5:-1], refs[-1]
    token[...] = jnp.zeros((8, 128), f32)
    other = jnp.where(place[1] == 0, place[2], place[0])
    for to in four:
        at = lax.rem(other + to, 4)
        for z in four:
            rows = pl.ds(pl.multiple_of(lax.rem(at, 2) * 896 + z * 224, 32), 224)
            out[to][224 * z : 224 * z + 224, :] = add([ref[lax.div(at, 2), rows, :] for ref in partial]).astype(bf16)
        for i in four:
            out[to][896 + 16 * i : 912 + 16 * i, :] = partial[i][0, 1792:1808, :]


def second_kernel(place, *refs):
    sums, out, held = refs[:4], refs[5:9], refs[9]
    x, core, y, z = [place[i] for i in four]
    for i in four:
        held[i] = sums[i][896:960, :].astype(f32)
    gain = jnp.zeros((4, 128), f32)
    for from_x in four:
        for from_y in four:
            back_x, back_y = lax.rem(x + 4 - from_x, 4), lax.rem(y + 4 - from_y, 4)
            major, other = jnp.where(core == 0, back_x, back_y), jnp.where(core == 0, back_y, back_x)
            gain = gain + gain_of(held[other, pl.ds(pl.multiple_of(major * 16, 16), 16), :])
    for to in four:
        rows = pl.ds(pl.multiple_of(lax.rem(z + to, 4) * 224, 32), 224)
        out[to][0:224, :] = add([ref[rows, :] for ref in sums]).astype(bf16)
        out[to][224:240, :] = gain_rows(gain)


def third_kernel(place, *refs):
    sums, weight_grad, gain_grad = refs[:4], *refs[4:]
    total = add([ref[0:224, :] for ref in sums])
    for i in four:
        weight_grad[:, lanes[i]] = total[56 * i : 56 * i + 56, :]
    gain_grad[...] = add([gain_of(ref[224:240, :]) for ref in sums])


def touch_kernel(value, token, out):
    out[...] = token[...] + value[0, 0:8, :].astype(f32)


def touch(value, token):
    return pl.pallas_call(
        touch_kernel,
        grid=(1,),
        in_specs=[pl.BlockSpec((1, 16, 128), lambda i: (0, 0, 0)), pl.BlockSpec((8, 128), lambda i: (0, 0))],
        out_specs=pl.BlockSpec((8, 128), lambda i: (0, 0)),
        out_shape=order,
        compiler_params=pltpu.CompilerParams(vmem_limit_bytes=4 * MIB),
        cost_estimate=pl.CostEstimate(flops=0, bytes_accessed=4096, transcendentals=0),
        name="touch",
    )(value, token)


def combine(kernel, shapes, place, values, scratch=(), tokens=()):
    vmem = pl.BlockSpec(memory_space=pltpu.VMEM)
    return pl.pallas_call(
        kernel,
        in_specs=[pl.BlockSpec(memory_space=pltpu.SMEM)]
        + [vmem] * (len(values) + len(tokens)),
        out_specs=[vmem] * len(shapes),
        out_shape=[jax.ShapeDtypeStruct(*shape) for shape in shapes],
        scratch_shapes=list(scratch),
        compiler_params=pltpu.CompilerParams(vmem_limit_bytes=24 * MIB),
        cost_estimate=pl.CostEstimate(flops=0, bytes_accessed=MIB, transcendentals=0),
        name=kernel.__name__,
    )(place, *values, *tokens)


def along_major(value, by):
    return fetch(value, lambda x, c, y, z: (x, c, y - by, z) if c else (x - by, c, y, z))


def along_other(value, by):
    return fetch(value, lambda x, c, y, z: (x - by, c, y, z) if c else (x, c, y - by, z))


def along_z(value, by):
    return fetch(value, lambda x, c, y, z: (x, c, y, z - by))


def exchange(values, along):
    return [values[0]] + [along(values[by], by) for by in (1, 2, 3)]


def first_sums(place, partial, latent_grad, gathered, token):
    sums = exchange(partial, along_major)
    input_grad, token = input_grads(latent_grad, gathered, token, 0, 4)
    token = touch(sums[1], touch(sums[2], token))
    outs = [((960, 128), bf16)] * 4 + [((8, 128), f32)]
    return combine(first_kernel, outs, place, sums, tokens=[token]), input_grad


def last_sums(place, sums, latent_grad, gathered, input_grad):
    token = sums[4]
    sums = exchange(sums[:4], along_other)
    input_grad, token = input_grads(latent_grad, gathered, token, 4, 3, [input_grad])
    scratch = [pltpu.VMEM((4, 64, 128), f32)]
    sums = combine(second_kernel, [((240, 128), bf16)] * 4, place, sums, scratch, [token])
    sums = exchange(sums, along_z)
    return *combine(third_kernel, [((56, 512), f32), ((4, 128), f32)], place, sums), input_grad


def shards(inputs, cotangent, weight, norm_gain):
    dp, shard = lax.axis_index("dp"), lax.axis_index("shard")
    core = dp % 2
    place = jnp.stack([dp // 2, core, shard // 4, shard % 4]).astype(jnp.int32)
    half = lax.dynamic_slice_in_dim(weight, core * 256, 256, 1)
    other_inputs = twin(inputs)
    kept, token = turn(place, inputs)
    line = join([half] + [fetch_first(half, by) for by in (1, 2, 3)], token)
    mine = [line] + [fetch_second(line, by) for by in (1, 2, 3)]
    other, token = turn(place, other_inputs)
    gain = norm_gain.reshape(1, 512)
    parts_of = functools.partial(latent_part, place, inputs)
    theirs = {0: twin(line)}
    first, _ = parts_of(mine[0], 0, 0)
    second, done = parts_of(theirs[0], 1, 0)
    mine[1] = tie(mine[1], token, done)
    theirs[1] = twin(mine[1])
    theirs[3] = twin(mine[3])
    first, _ = parts_of(mine[1], 0, 1, first)
    first, done = parts_of(mine[3], 0, 3, first)
    second, _ = parts_of(theirs[1], 1, 1, second)
    second, after = parts_of(theirs[3], 1, 3, second)
    mine[2] = tie(mine[2], done, after)
    theirs[2] = twin(mine[2])
    first, _ = parts_of(mine[2], 0, 2, first)
    second, _ = parts_of(theirs[2], 1, 2, second, (first, cotangent, gain))
    theirs = [theirs[i] for i in four]
    latent_grad = second
    other_grad = twin(latent_grad)
    partial, tokens = [None] * 4, []
    for by in (2, 1, 3, 0):
        partial[by], token = weight_grads(place, kept, other, latent_grad, other_grad, by, tokens)
        tokens = [token]
    gathered = assemble(place, mine + theirs, token)
    sums, input_grad = first_sums(place, partial, latent_grad, gathered, token)
    weight_grad, gain_grad, input_grad = last_sums(place, sums, latent_grad, gathered, input_grad)
    return (input_grad, weight_grad, gain_grad.reshape(512))


def solution(mesh):
    placed = (P(("dp", "shard"), None), P(("dp", "shard"), None), P("shard", None), P())
    return jax.shard_map(
        shards,
        mesh=mesh,
        in_specs=placed,
        out_specs=(P(("dp", "shard"), None), P(("dp", "shard"), None), P()),
        check_vma=False,
    )
```

```python
import functools

import jax
import jax.numpy as jnp
from jax import lax
from jax.experimental import pallas as pl
from jax.experimental.pallas import tpu as pltpu
from jax.sharding import PartitionSpec as P

epsilon = 1e-06
axes = ("dp", "shard")
bf16, f32 = jnp.bfloat16, jnp.float32
MIB = 1024 * 1024


def device(x, core, y, z):
    return ((x % 4) * 2 + core) * 16 + (y % 4) * 4 + z % 4


four = range(4)
spots = [(x, c, y, z) for x in four for c in range(2) for y in four for z in four]


def fetch(value, source):
    return lax.ppermute(value, axes, [(device(*source(*spot)), device(*spot)) for spot in spots])


def twin(value):
    return fetch(value, lambda x, c, y, z: (x, 1 - c, y, z))


def fetch_first(value, by):
    return fetch(value, lambda x, c, y, z: (x, c, y, z + by) if c else (x, c, y + by, z))


def fetch_second(value, by):
    return fetch(value, lambda x, c, y, z: (x, c, y + by, z) if c else (x, c, y, z + by))


order = jax.ShapeDtypeStruct((8, 128), f32)


def turn_kernel(place, rows, out, token):
    token[...] = jnp.zeros((8, 128), f32)
    for column in range(0, 896, 128):
        out[column : column + 128, :] = rows[:, column : column + 128].T


def turn(place, inputs):
    return pl.pallas_call(
        turn_kernel,
        grid_spec=pltpu.PrefetchScalarGridSpec(
            num_scalar_prefetch=1,
            grid=(4,),
            in_specs=[pl.BlockSpec((768, 896), lambda i, place: (0, 2 * i + place[1]))],
            out_specs=[
                pl.BlockSpec((896, 768), lambda i, place: (i, 0)),
                pl.BlockSpec((8, 128), lambda i, place: (0, 0)),
            ],
        ),
        out_shape=[jax.ShapeDtypeStruct((3584, 768), bf16), order],
        compiler_params=pltpu.CompilerParams(vmem_limit_bytes=16 * MIB),
        cost_estimate=pl.CostEstimate(flops=0, bytes_accessed=22 * MIB, transcendentals=0),
        name="turn",
    )(place, inputs)


def tie_kernel(value, *refs):
    refs[-1][...] = value[...]


def tie(value, *tokens):
    vmem = pl.BlockSpec(memory_space=pltpu.VMEM)
    return pl.pallas_call(
        tie_kernel,
        in_specs=[vmem] * (1 + len(tokens)),
        out_specs=vmem,
        out_shape=jax.ShapeDtypeStruct(value.shape, value.dtype),
        compiler_params=pltpu.CompilerParams(vmem_limit_bytes=8 * MIB),
        cost_estimate=pl.CostEstimate(flops=0, bytes_accessed=4096, transcendentals=0),
        name="tie",
    )(value, *tokens)


def join_kernel(one, two, three, four_, token, out):
    for i, ref in enumerate((one, two, three, four_)):
        out[i] = ref[...]


def join(values, token):
    vmem = pl.BlockSpec(memory_space=pltpu.VMEM)
    return pl.pallas_call(
        join_kernel,
        in_specs=[vmem] * 5,
        out_specs=vmem,
        out_shape=jax.ShapeDtypeStruct((4, 448, 256), bf16),
        compiler_params=pltpu.CompilerParams(vmem_limit_bytes=8 * MIB),
        cost_estimate=pl.CostEstimate(flops=0, bytes_accessed=2 * MIB, transcendentals=0),
        name="join",
    )(*values, token)


def spot(place, side, far, near):
    part = place[1] if side == 0 else 1 - place[1]
    along_y = lax.rem(place[2] + jnp.where(part == 0, near, far), 4)
    along_z = lax.rem(place[3] + jnp.where(part == 0, far, near), 4)
    return along_y * 4 + along_z, part


def norm(place, start, sums, first, second, cotangent, gain, out):
    core = place[1]
    own = pl.ds(pl.multiple_of(core * 256, 256), 256)
    other = pl.ds(pl.multiple_of(256 - core * 256, 256), 256)

    for i in range(4):
        tokens = pl.ds(start + i * 64, 64)
        latent = [first[tokens, :], second[tokens, :]]
        square = sum(jnp.sum(value * value, axis=1, keepdims=True) for value in latent)
        scale = lax.rsqrt(square * (1.0 / 512) + epsilon)
        normed = [value * scale for value in latent]
        upstream = [cotangent[tokens, lane].astype(f32) for lane in (own, other)]
        scaled = [value * gain[:, lane] for value, lane in zip(upstream, (own, other))]
        center = sum(jnp.sum(u * v, axis=1, keepdims=True) for u, v in zip(scaled, normed)) * (1.0 / 512)
        for lane, u, v in zip((own, other), scaled, normed):
            out[tokens, lane] = (scale * (u - v * center)).astype(bf16)
        sums = tuple(
            total + jnp.sum((u * v).reshape(8, 8, 256), axis=0) for total, u, v in zip(sums, upstream, normed)
        )
    return sums


def norm_gain_rows(place, sums, out, row):
    core = place[1]
    for half, value in zip((core, 1 - core), sums):
        lane = pl.ds(pl.multiple_of(half * 256, 256), 256)
        row[:, lane] = jnp.broadcast_to(jnp.sum(value, axis=0, keepdims=True), (8, 256))
    out[768:784, :] = split(row[0:1, :])


def latent_kernel(side, far, has_before, last, place, inputs, piece, *refs):
    at = 1 * has_before
    ending = refs[at : at + 3 * last]
    out, token, filled, window, arrive, *extra = refs[at + 3 * last :]
    token[...] = jnp.zeros((8, 128), f32)
    total = extra[0] if last else out
    copies = []
    for near in four:
        block, part = spot(place, side, far, near)
        first = pl.multiple_of(lax.div(block * 7, 2) * 128, 128)
        copy = pltpu.make_async_copy(
            inputs.at[:, pl.ds(first, 512)], window.at[:, 512 * near : 512 * near + 512], arrive.at[near]
        )
        copy.start()
        copies.append(copy)
    for near in four:
        block, part = spot(place, side, far, near)
        odd = lax.rem(block, 2)
        filled[pl.ds(pl.multiple_of(512 * near + odd * 64, 64), 448), :] = piece[near]
        filled[pl.ds(pl.multiple_of(512 * near + 448 - odd * 448, 64), 64), :] = jnp.zeros((64, 256), bf16)
    for copy in copies:
        copy.wait()
    sums = (jnp.zeros((8, 256), f32),) * 2
    for start in range(0, 768, 256):
        product = jnp.dot(window[start : start + 256, :], filled[...], preferred_element_type=f32)
        total[start : start + 256, :] = refs[0][start : start + 256, :] + product if has_before else product
        if last:
            sums = norm(place, start, sums, ending[0], total, ending[1], ending[2], out)
    if last:
        norm_gain_rows(place, sums, out, extra[1])


def latent_part(place, inputs, piece, side, far, before=None, ending=()):
    hbm, vmem = pl.BlockSpec(memory_space=pltpu.HBM), pl.BlockSpec(memory_space=pltpu.VMEM)
    last = len(ending) > 0
    operands = [place, inputs, piece] + ([] if before is None else [before]) + list(ending)
    specs = [pl.BlockSpec(memory_space=pltpu.SMEM), hbm] + [vmem] * (len(operands) - 2)
    scratch = [pltpu.VMEM((2048, 256), bf16), pltpu.VMEM((768, 2048), bf16), pltpu.SemaphoreType.DMA((4,))]
    out = jax.ShapeDtypeStruct((768, 256), f32)
    if last:
        scratch += [pltpu.VMEM((768, 256), f32), pltpu.VMEM((8, 512), f32)]
        out = jax.ShapeDtypeStruct((784, 512), bf16)
    return pl.pallas_call(
        functools.partial(latent_kernel, side, far, before is not None, last),
        in_specs=specs,
        out_specs=[vmem] * 2,
        scratch_shapes=scratch,
        out_shape=[out, order],
        compiler_params=pltpu.CompilerParams(vmem_limit_bytes=14 * MIB),
        cost_estimate=pl.CostEstimate(flops=0, bytes_accessed=4096, transcendentals=0),
        name="latent",
    )(*operands)


def assemble_kernel(place, *refs):
    out = refs[9]
    for side in range(2):
        for far in four:
            for near in four:
                block, part = spot(place, side, far, near)
                rows = pl.ds(pl.multiple_of(block * 448, 64), 448)
                columns = pl.ds(pl.multiple_of(part * 256, 256), 256)
                out[rows, columns] = refs[side * 4 + far][near]


def assemble(place, pieces, token):
    vmem = pl.BlockSpec(memory_space=pltpu.VMEM)
    return pl.pallas_call(
        assemble_kernel,
        in_specs=[pl.BlockSpec(memory_space=pltpu.SMEM)] + [vmem] * 9,
        out_specs=vmem,
        out_shape=jax.ShapeDtypeStruct((7168, 512), bf16),
        compiler_params=pltpu.CompilerParams(vmem_limit_bytes=20 * MIB),
        cost_estimate=pl.CostEstimate(flops=0, bytes_accessed=MIB, transcendentals=0),
        name="assemble",
    )(place, *pieces, token)


def parts(value):
    high = value.astype(bf16).astype(f32)
    middle = (value - high).astype(bf16).astype(f32)
    return [high, middle, value - high - middle]


def split(value):
    return jnp.concatenate(parts(value) + [jnp.zeros((13, 512), f32)], axis=0).astype(bf16)


def total_of(rows):
    return jnp.sum(rows[768:784, :].astype(f32), axis=0, keepdims=True)


def input_kernel(grad, weight, before, *refs):
    out, token = refs[-2:]
    token[...] = jnp.zeros((8, 128), f32)
    out[...] = lax.dot_general(
        grad[:768, :], weight[...], (((1,), (1,)), ((), ())), preferred_element_type=f32
    ).astype(bf16)


def input_grads(grad, weight, token, first, count, begun=()):
    small = pl.BlockSpec((8, 128), lambda i: (0, 0))
    return pl.pallas_call(
        input_kernel,
        grid=(count,),
        in_specs=[
            pl.BlockSpec((784, 512), lambda i: (0, 0)),
            pl.BlockSpec((1024, 512), lambda i: (first + i, 0)),
            small,
        ]
        + [pl.BlockSpec(memory_space=pltpu.HBM)] * len(begun),
        out_specs=[pl.BlockSpec((768, 1024), lambda i: (0, first + i)), small],
        out_shape=[jax.ShapeDtypeStruct((768, 7168), bf16), order],
        input_output_aliases={3: 0} if begun else {},
        compiler_params=pltpu.CompilerParams(vmem_limit_bytes=40 * MIB),
        cost_estimate=pl.CostEstimate(flops=0, bytes_accessed=MIB, transcendentals=0),
        name="input_grads",
    )(grad, weight, token, *begun)


lanes = [slice(128 * i, 128 * i + 128) for i in four]


def flat(rows):
    return jnp.concatenate([rows[:, lane] for lane in lanes], axis=0)


def weight_kernel(place, *refs):
    mine, other, mine_grad, other_grad = refs[:2], refs[2:4], *refs[4:6]
    out, token, held = refs[-3:]
    token[...] = jnp.zeros((8, 128), f32)
    rows = jnp.concatenate([mine[0][...], mine[1][...]], axis=0)
    product = jnp.dot(rows, mine_grad[:768, :], preferred_element_type=f32)
    rows = jnp.concatenate([other[0][...], other[1][...]], axis=0)
    product += jnp.dot(rows, other_grad[:768, :], preferred_element_type=f32)
    held[...] = product.reshape(8, 56, 512)
    for i in range(8):
        out[0, 224 * i : 224 * i + 224, :] = flat(held[i]).astype(bf16)
    gain = total_of(mine_grad) + total_of(other_grad)
    out[0, 1792:1808, :] = gain_rows(flat(gain))


def gain_rows(gain):
    return jnp.concatenate(parts(gain) + [jnp.zeros((4, 128), f32)], axis=0).astype(bf16)


def gain_of(rows):
    rows = rows.astype(f32)
    return (rows[0:4] + rows[4:8]) + rows[8:12]


def weight_grads(place, mine, other, mine_grad, other_grad, by, tokens):
    def rows(i):
        def index(pair, place):
            x_ahead = lax.rem(place[0] + by, 4) * 4 + pair * 2 + i
            y_ahead = (pair * 2 + i) * 4 + lax.rem(place[2] + by, 4)
            return jnp.where(place[1] == 0, x_ahead, y_ahead), 0

        return pl.BlockSpec((224, 768), index)

    whole = pl.BlockSpec((784, 512), lambda pair, place: (0, 0))
    small = pl.BlockSpec((8, 128), lambda pair, place: (0, 0))
    return pl.pallas_call(
        weight_kernel,
        grid_spec=pltpu.PrefetchScalarGridSpec(
            num_scalar_prefetch=1,
            grid=(2,),
            in_specs=[rows(0), rows(1)] * 2 + [whole] * 2 + [small] * len(tokens),
            out_specs=[pl.BlockSpec((1, 1808, 128), lambda pair, place: (pair, 0, 0)), small],
            scratch_shapes=[pltpu.VMEM((8, 56, 512), f32)],
        ),
        out_shape=[jax.ShapeDtypeStruct((2, 1808, 128), bf16), order],
        compiler_params=pltpu.CompilerParams(vmem_limit_bytes=14 * MIB),
        cost_estimate=pl.CostEstimate(flops=0, bytes_accessed=MIB, transcendentals=0),
        name="weight_grads",
    )(place, mine, mine, other, other, mine_grad, other_grad, *tokens)


def add(values):
    own, one, two, three = [value.astype(f32) for value in values]
    return (own + two) + (one + three)


def first_kernel(place, *refs):
    partial, out, token = refs[:4], refs[-5:-1], refs[-1]
    token[...] = jnp.zeros((8, 128), f32)
    other = jnp.where(place[1] == 0, place[2], place[0])
    for to in four:
        at = lax.rem(other + to, 4)
        for z in four:
            rows = pl.ds(pl.multiple_of(lax.rem(at, 2) * 896 + z * 224, 32), 224)
            out[to][224 * z : 224 * z + 224, :] = add([ref[lax.div(at, 2), rows, :] for ref in partial]).astype(bf16)
        for i in four:
            out[to][896 + 16 * i : 912 + 16 * i, :] = partial[i][0, 1792:1808, :]


def second_kernel(place, *refs):
    sums, out, held = refs[:4], refs[5:9], refs[9]
    x, core, y, z = [place[i] for i in four]
    for i in four:
        held[i] = sums[i][896:960, :].astype(f32)
    gain = jnp.zeros((4, 128), f32)
    for from_x in four:
        for from_y in four:
            back_x, back_y = lax.rem(x + 4 - from_x, 4), lax.rem(y + 4 - from_y, 4)
            major, other = jnp.where(core == 0, back_x, back_y), jnp.where(core == 0, back_y, back_x)
            gain = gain + gain_of(held[other, pl.ds(pl.multiple_of(major * 16, 16), 16), :])
    for to in four:
        rows = pl.ds(pl.multiple_of(lax.rem(z + to, 4) * 224, 32), 224)
        out[to][0:224, :] = add([ref[rows, :] for ref in sums]).astype(bf16)
        out[to][224:240, :] = gain_rows(gain)


def third_kernel(place, *refs):
    sums, weight_grad, gain_grad = refs[:4], *refs[4:]
    total = add([ref[0:224, :] for ref in sums])
    for i in four:
        weight_grad[:, lanes[i]] = total[56 * i : 56 * i + 56, :]
    gain_grad[...] = add([gain_of(ref[224:240, :]) for ref in sums])


def touch_kernel(value, token, out):
    out[...] = token[...] + value[0, 0:8, :].astype(f32)


def touch(value, token):
    return pl.pallas_call(
        touch_kernel,
        grid=(1,),
        in_specs=[pl.BlockSpec((1, 16, 128), lambda i: (0, 0, 0)), pl.BlockSpec((8, 128), lambda i: (0, 0))],
        out_specs=pl.BlockSpec((8, 128), lambda i: (0, 0)),
        out_shape=order,
        compiler_params=pltpu.CompilerParams(vmem_limit_bytes=4 * MIB),
        cost_estimate=pl.CostEstimate(flops=0, bytes_accessed=4096, transcendentals=0),
        name="touch",
    )(value, token)


def combine(kernel, shapes, place, values, scratch=(), tokens=()):
    vmem = pl.BlockSpec(memory_space=pltpu.VMEM)
    return pl.pallas_call(
        kernel,
        in_specs=[pl.BlockSpec(memory_space=pltpu.SMEM)]
        + [vmem] * (len(values) + len(tokens)),
        out_specs=[vmem] * len(shapes),
        out_shape=[jax.ShapeDtypeStruct(*shape) for shape in shapes],
        scratch_shapes=list(scratch),
        compiler_params=pltpu.CompilerParams(vmem_limit_bytes=24 * MIB),
        cost_estimate=pl.CostEstimate(flops=0, bytes_accessed=MIB, transcendentals=0),
        name=kernel.__name__,
    )(place, *values, *tokens)


def along_major(value, by):
    return fetch(value, lambda x, c, y, z: (x, c, y - by, z) if c else (x - by, c, y, z))


def along_other(value, by):
    return fetch(value, lambda x, c, y, z: (x - by, c, y, z) if c else (x, c, y - by, z))


def along_z(value, by):
    return fetch(value, lambda x, c, y, z: (x, c, y, z - by))


def exchange(values, along):
    return [values[0]] + [along(values[by], by) for by in (1, 2, 3)]


def first_sums(place, partial, latent_grad, gathered, token):
    sums = exchange(partial, along_major)
    input_grad, token = input_grads(latent_grad, gathered, token, 0, 4)
    token = touch(sums[1], touch(sums[2], token))
    outs = [((960, 128), bf16)] * 4 + [((8, 128), f32)]
    return combine(first_kernel, outs, place, sums, tokens=[token]), input_grad


def last_sums(place, sums, latent_grad, gathered, input_grad):
    token = sums[4]
    sums = exchange(sums[:4], along_other)
    input_grad, token = input_grads(latent_grad, gathered, token, 4, 3, [input_grad])
    scratch = [pltpu.VMEM((4, 64, 128), f32)]
    sums = combine(second_kernel, [((240, 128), bf16)] * 4, place, sums, scratch, [token])
    sums = exchange(sums, along_z)
    return *combine(third_kernel, [((56, 512), f32), ((4, 128), f32)], place, sums), input_grad


def shards(inputs, cotangent, weight, norm_gain):
    dp, shard = lax.axis_index("dp"), lax.axis_index("shard")
    core = dp % 2
    place = jnp.stack([dp // 2, core, shard // 4, shard % 4]).astype(jnp.int32)
    half = lax.dynamic_slice_in_dim(weight, core * 256, 256, 1)
    other_inputs = twin(inputs)
    kept, token = turn(place, inputs)
    line = join([half] + [fetch_first(half, by) for by in (1, 2, 3)], token)
    mine = [line] + [fetch_second(line, by) for by in (1, 2, 3)]
    other, token = turn(place, other_inputs)
    gain = norm_gain.reshape(1, 512)
    parts_of = functools.partial(latent_part, place, inputs)
    theirs = {0: twin(line)}
    first, _ = parts_of(mine[0], 0, 0)
    second, done = parts_of(theirs[0], 1, 0)
    mine[1] = tie(mine[1], token, done)
    theirs[1] = twin(mine[1])
    theirs[3] = twin(mine[3])
    first, _ = parts_of(mine[1], 0, 1, first)
    first, done = parts_of(mine[3], 0, 3, first)
    second, _ = parts_of(theirs[1], 1, 1, second)
    second, after = parts_of(theirs[3], 1, 3, second)
    mine[2] = tie(mine[2], done, after)
    theirs[2] = twin(mine[2])
    first, _ = parts_of(mine[2], 0, 2, first)
    second, _ = parts_of(theirs[2], 1, 2, second, (first, cotangent, gain))
    theirs = [theirs[i] for i in four]
    latent_grad = second
    other_grad = twin(latent_grad)
    partial, tokens = [None] * 4, []
    for by in (2, 1, 3, 0):
        partial[by], token = weight_grads(place, kept, other, latent_grad, other_grad, by, tokens)
        tokens = [token]
    gathered = assemble(place, mine + theirs, token)
    sums, input_grad = first_sums(place, partial, latent_grad, gathered, token)
    weight_grad, gain_grad, input_grad = last_sums(place, sums, latent_grad, gathered, input_grad)
    return (input_grad, weight_grad, gain_grad.reshape(512))


def solution(mesh):
    placed = (P(("dp", "shard"), None), P(("dp", "shard"), None), P("shard", None), P())
    return jax.shard_map(
        shards,
        mesh=mesh,
        in_specs=placed,
        out_specs=(P(("dp", "shard"), None), P(("dp", "shard"), None), P()),
        check_vma=False,
    )
```

```python
import functools

import jax
import jax.numpy as jnp
from jax import lax
from jax.experimental import pallas as pl
from jax.experimental.pallas import tpu as pltpu
from jax.sharding import PartitionSpec as P

epsilon = 1e-06
axes = ("dp", "shard")
bf16, f32 = jnp.bfloat16, jnp.float32
MIB = 1024 * 1024


def device(x, core, y, z):
    return ((x % 4) * 2 + core) * 16 + (y % 4) * 4 + z % 4


four = range(4)
spots = [(x, c, y, z) for x in four for c in range(2) for y in four for z in four]


def fetch(value, source):
    return lax.ppermute(value, axes, [(device(*source(*spot)), device(*spot)) for spot in spots])


def twin(value):
    return fetch(value, lambda x, c, y, z: (x, 1 - c, y, z))


def fetch_first(value, by):
    return fetch(value, lambda x, c, y, z: (x, c, y, z + by) if c else (x, c, y + by, z))


def fetch_second(value, by):
    return fetch(value, lambda x, c, y, z: (x, c, y + by, z) if c else (x, c, y, z + by))


order = jax.ShapeDtypeStruct((8, 128), f32)


def turn_kernel(place, rows, out, token):
    token[...] = jnp.zeros((8, 128), f32)
    for column in range(0, 896, 128):
        out[column : column + 128, :] = rows[:, column : column + 128].T


def turn(place, inputs):
    return pl.pallas_call(
        turn_kernel,
        grid_spec=pltpu.PrefetchScalarGridSpec(
            num_scalar_prefetch=1,
            grid=(4,),
            in_specs=[pl.BlockSpec((768, 896), lambda i, place: (0, 2 * i + place[1]))],
            out_specs=[
                pl.BlockSpec((896, 768), lambda i, place: (i, 0)),
                pl.BlockSpec((8, 128), lambda i, place: (0, 0)),
            ],
        ),
        out_shape=[jax.ShapeDtypeStruct((3584, 768), bf16), order],
        compiler_params=pltpu.CompilerParams(vmem_limit_bytes=16 * MIB),
        cost_estimate=pl.CostEstimate(flops=0, bytes_accessed=22 * MIB, transcendentals=0),
        name="turn",
    )(place, inputs)


def tie_kernel(value, *refs):
    refs[-1][...] = value[...]


def tie(value, *tokens):
    vmem = pl.BlockSpec(memory_space=pltpu.VMEM)
    return pl.pallas_call(
        tie_kernel,
        in_specs=[vmem] * (1 + len(tokens)),
        out_specs=vmem,
        out_shape=jax.ShapeDtypeStruct(value.shape, value.dtype),
        compiler_params=pltpu.CompilerParams(vmem_limit_bytes=8 * MIB),
        cost_estimate=pl.CostEstimate(flops=0, bytes_accessed=4096, transcendentals=0),
        name="tie",
    )(value, *tokens)


def join_kernel(one, two, three, four_, token, out):
    for i, ref in enumerate((one, two, three, four_)):
        out[i] = ref[...]


def join(values, token):
    vmem = pl.BlockSpec(memory_space=pltpu.VMEM)
    return pl.pallas_call(
        join_kernel,
        in_specs=[vmem] * 5,
        out_specs=vmem,
        out_shape=jax.ShapeDtypeStruct((4, 448, 256), bf16),
        compiler_params=pltpu.CompilerParams(vmem_limit_bytes=8 * MIB),
        cost_estimate=pl.CostEstimate(flops=0, bytes_accessed=2 * MIB, transcendentals=0),
        name="join",
    )(*values, token)


def spot(place, side, far, near):
    part = place[1] if side == 0 else 1 - place[1]
    along_y = lax.rem(place[2] + jnp.where(part == 0, near, far), 4)
    along_z = lax.rem(place[3] + jnp.where(part == 0, far, near), 4)
    return along_y * 4 + along_z, part


def norm(place, start, sums, first, second, cotangent, gain, out):
    core = place[1]
    own = pl.ds(pl.multiple_of(core * 256, 256), 256)
    other = pl.ds(pl.multiple_of(256 - core * 256, 256), 256)

    for i in range(4):
        tokens = pl.ds(start + i * 64, 64)
        latent = [first[tokens, :], second[tokens, :]]
        square = sum(jnp.sum(value * value, axis=1, keepdims=True) for value in latent)
        scale = lax.rsqrt(square * (1.0 / 512) + epsilon)
        normed = [value * scale for value in latent]
        upstream = [cotangent[tokens, lane].astype(f32) for lane in (own, other)]
        scaled = [value * gain[:, lane] for value, lane in zip(upstream, (own, other))]
        center = sum(jnp.sum(u * v, axis=1, keepdims=True) for u, v in zip(scaled, normed)) * (1.0 / 512)
        for lane, u, v in zip((own, other), scaled, normed):
            out[tokens, lane] = (scale * (u - v * center)).astype(bf16)
        sums = tuple(
            total + jnp.sum((u * v).reshape(8, 8, 256), axis=0) for total, u, v in zip(sums, upstream, normed)
        )
    return sums


def norm_gain_rows(place, sums, out, row):
    core = place[1]
    for half, value in zip((core, 1 - core), sums):
        lane = pl.ds(pl.multiple_of(half * 256, 256), 256)
        row[:, lane] = jnp.broadcast_to(jnp.sum(value, axis=0, keepdims=True), (8, 256))
    out[768:784, :] = split(row[0:1, :])


def latent_kernel(side, far, has_before, last, place, inputs, piece, *refs):
    at = 1 * has_before
    ending = refs[at : at + 3 * last]
    out, token, filled, window, arrive, *extra = refs[at + 3 * last :]
    token[...] = jnp.zeros((8, 128), f32)
    total = extra[0] if last else out
    copies = []
    for near in four:
        block, part = spot(place, side, far, near)
        first = pl.multiple_of(lax.div(block * 7, 2) * 128, 128)
        copy = pltpu.make_async_copy(
            inputs.at[:, pl.ds(first, 512)], window.at[:, 512 * near : 512 * near + 512], arrive.at[near]
        )
        copy.start()
        copies.append(copy)
    for near in four:
        block, part = spot(place, side, far, near)
        odd = lax.rem(block, 2)
        filled[pl.ds(pl.multiple_of(512 * near + odd * 64, 64), 448), :] = piece[near]
        filled[pl.ds(pl.multiple_of(512 * near + 448 - odd * 448, 64), 64), :] = jnp.zeros((64, 256), bf16)
    for copy in copies:
        copy.wait()
    sums = (jnp.zeros((8, 256), f32),) * 2
    for start in range(0, 768, 256):
        product = jnp.dot(window[start : start + 256, :], filled[...], preferred_element_type=f32)
        total[start : start + 256, :] = refs[0][start : start + 256, :] + product if has_before else product
        if last:
            sums = norm(place, start, sums, ending[0], total, ending[1], ending[2], out)
    if last:
        norm_gain_rows(place, sums, out, extra[1])


def latent_part(place, inputs, piece, side, far, before=None, ending=()):
    hbm, vmem = pl.BlockSpec(memory_space=pltpu.HBM), pl.BlockSpec(memory_space=pltpu.VMEM)
    last = len(ending) > 0
    operands = [place, inputs, piece] + ([] if before is None else [before]) + list(ending)
    specs = [pl.BlockSpec(memory_space=pltpu.SMEM), hbm] + [vmem] * (len(operands) - 2)
    scratch = [pltpu.VMEM((2048, 256), bf16), pltpu.VMEM((768, 2048), bf16), pltpu.SemaphoreType.DMA((4,))]
    out = jax.ShapeDtypeStruct((768, 256), f32)
    if last:
        scratch += [pltpu.VMEM((768, 256), f32), pltpu.VMEM((8, 512), f32)]
        out = jax.ShapeDtypeStruct((784, 512), bf16)
    return pl.pallas_call(
        functools.partial(latent_kernel, side, far, before is not None, last),
        in_specs=specs,
        out_specs=[vmem] * 2,
        scratch_shapes=scratch,
        out_shape=[out, order],
        compiler_params=pltpu.CompilerParams(vmem_limit_bytes=14 * MIB),
        cost_estimate=pl.CostEstimate(flops=0, bytes_accessed=4096, transcendentals=0),
        name="latent",
    )(*operands)


def assemble_kernel(place, *refs):
    out = refs[9]
    for side in range(2):
        for far in four:
            for near in four:
                block, part = spot(place, side, far, near)
                rows = pl.ds(pl.multiple_of(block * 448, 64), 448)
                columns = pl.ds(pl.multiple_of(part * 256, 256), 256)
                out[rows, columns] = refs[side * 4 + far][near]


def assemble(place, pieces, token):
    vmem = pl.BlockSpec(memory_space=pltpu.VMEM)
    return pl.pallas_call(
        assemble_kernel,
        in_specs=[pl.BlockSpec(memory_space=pltpu.SMEM)] + [vmem] * 9,
        out_specs=vmem,
        out_shape=jax.ShapeDtypeStruct((7168, 512), bf16),
        compiler_params=pltpu.CompilerParams(vmem_limit_bytes=20 * MIB),
        cost_estimate=pl.CostEstimate(flops=0, bytes_accessed=MIB, transcendentals=0),
        name="assemble",
    )(place, *pieces, token)


def parts(value):
    high = value.astype(bf16).astype(f32)
    middle = (value - high).astype(bf16).astype(f32)
    return [high, middle, value - high - middle]


def split(value):
    return jnp.concatenate(parts(value) + [jnp.zeros((13, 512), f32)], axis=0).astype(bf16)


def total_of(rows):
    return jnp.sum(rows[768:784, :].astype(f32), axis=0, keepdims=True)


def input_kernel(grad, weight, before, *refs):
    out, token = refs[-2:]
    token[...] = jnp.zeros((8, 128), f32)
    out[...] = lax.dot_general(
        grad[:768, :], weight[...], (((1,), (1,)), ((), ())), preferred_element_type=f32
    ).astype(bf16)


def input_grads(grad, weight, token):
    small = pl.BlockSpec((8, 128), lambda i: (0, 0))
    return pl.pallas_call(
        input_kernel,
        grid=(7,),
        in_specs=[
            pl.BlockSpec((784, 512), lambda i: (0, 0)),
            pl.BlockSpec((1024, 512), lambda i: (i, 0)),
            small,
        ],
        out_specs=[pl.BlockSpec((768, 1024), lambda i: (0, i)), small],
        out_shape=[jax.ShapeDtypeStruct((768, 7168), bf16), order],
        compiler_params=pltpu.CompilerParams(vmem_limit_bytes=40 * MIB),
        cost_estimate=pl.CostEstimate(flops=0, bytes_accessed=MIB, transcendentals=0),
        name="input_grads",
    )(grad, weight, token)


lanes = [slice(128 * i, 128 * i + 128) for i in four]


def flat(rows):
    return jnp.concatenate([rows[:, lane] for lane in lanes], axis=0)


def weight_kernel(place, *refs):
    mine, other, mine_grad, other_grad = refs[:2], refs[2:4], *refs[4:6]
    out, token, held = refs[-3:]
    token[...] = jnp.zeros((8, 128), f32)
    rows = jnp.concatenate([mine[0][...], mine[1][...]], axis=0)
    product = jnp.dot(rows, mine_grad[:768, :], preferred_element_type=f32)
    rows = jnp.concatenate([other[0][...], other[1][...]], axis=0)
    product += jnp.dot(rows, other_grad[:768, :], preferred_element_type=f32)
    held[...] = product.reshape(8, 56, 512)
    for i in range(8):
        out[0, 224 * i : 224 * i + 224, :] = flat(held[i]).astype(bf16)
    gain = total_of(mine_grad) + total_of(other_grad)
    out[0, 1792:1808, :] = gain_rows(flat(gain))


def gain_rows(gain):
    return jnp.concatenate(parts(gain) + [jnp.zeros((4, 128), f32)], axis=0).astype(bf16)


def gain_of(rows):
    rows = rows.astype(f32)
    return (rows[0:4] + rows[4:8]) + rows[8:12]


def weight_grads(place, mine, other, mine_grad, other_grad, by, tokens):
    def rows(i):
        def index(pair, place):
            x_ahead = lax.rem(place[0] + by, 4) * 4 + pair * 2 + i
            y_ahead = (pair * 2 + i) * 4 + lax.rem(place[2] + by, 4)
            return jnp.where(place[1] == 0, x_ahead, y_ahead), 0

        return pl.BlockSpec((224, 768), index)

    whole = pl.BlockSpec((784, 512), lambda pair, place: (0, 0))
    small = pl.BlockSpec((8, 128), lambda pair, place: (0, 0))
    return pl.pallas_call(
        weight_kernel,
        grid_spec=pltpu.PrefetchScalarGridSpec(
            num_scalar_prefetch=1,
            grid=(2,),
            in_specs=[rows(0), rows(1)] * 2 + [whole] * 2 + [small] * len(tokens),
            out_specs=[pl.BlockSpec((1, 1808, 128), lambda pair, place: (pair, 0, 0)), small],
            scratch_shapes=[pltpu.VMEM((8, 56, 512), f32)],
        ),
        out_shape=[jax.ShapeDtypeStruct((2, 1808, 128), bf16), order],
        compiler_params=pltpu.CompilerParams(vmem_limit_bytes=14 * MIB),
        cost_estimate=pl.CostEstimate(flops=0, bytes_accessed=MIB, transcendentals=0),
        name="weight_grads",
    )(place, mine, mine, other, other, mine_grad, other_grad, *tokens)


def add(values):
    own, one, two, three = [value.astype(f32) for value in values]
    return (own + two) + (one + three)


def first_kernel(place, *refs):
    partial, out = refs[:4], refs[-4:]
    other = jnp.where(place[1] == 0, place[2], place[0])
    for to in four:
        at = lax.rem(other + to, 4)
        for z in four:
            rows = pl.ds(pl.multiple_of(lax.rem(at, 2) * 896 + z * 224, 32), 224)
            out[to][224 * z : 224 * z + 224, :] = add([ref[lax.div(at, 2), rows, :] for ref in partial]).astype(bf16)
        for i in four:
            out[to][896 + 16 * i : 912 + 16 * i, :] = partial[i][0, 1792:1808, :]


def second_kernel(place, *refs):
    sums, out, held = refs[:4], refs[4:8], refs[8]
    x, core, y, z = [place[i] for i in four]
    for i in four:
        held[i] = sums[i][896:960, :].astype(f32)
    gain = jnp.zeros((4, 128), f32)
    for from_x in four:
        for from_y in four:
            back_x, back_y = lax.rem(x + 4 - from_x, 4), lax.rem(y + 4 - from_y, 4)
            major, other = jnp.where(core == 0, back_x, back_y), jnp.where(core == 0, back_y, back_x)
            gain = gain + gain_of(held[other, pl.ds(pl.multiple_of(major * 16, 16), 16), :])
    for to in four:
        rows = pl.ds(pl.multiple_of(lax.rem(z + to, 4) * 224, 32), 224)
        out[to][0:224, :] = add([ref[rows, :] for ref in sums]).astype(bf16)
        out[to][224:240, :] = gain_rows(gain)


def third_kernel(place, *refs):
    sums, weight_grad, gain_grad = refs[:4], *refs[4:]
    total = add([ref[0:224, :] for ref in sums])
    for i in four:
        weight_grad[:, lanes[i]] = total[56 * i : 56 * i + 56, :]
    gain_grad[...] = add([gain_of(ref[224:240, :]) for ref in sums])


def touch_kernel(value, token, out):
    out[...] = token[...] + value[0, 0:8, :].astype(f32)


def touch(value, token):
    return pl.pallas_call(
        touch_kernel,
        grid=(1,),
        in_specs=[pl.BlockSpec((1, 16, 128), lambda i: (0, 0, 0)), pl.BlockSpec((8, 128), lambda i: (0, 0))],
        out_specs=pl.BlockSpec((8, 128), lambda i: (0, 0)),
        out_shape=order,
        compiler_params=pltpu.CompilerParams(vmem_limit_bytes=4 * MIB),
        cost_estimate=pl.CostEstimate(flops=0, bytes_accessed=4096, transcendentals=0),
        name="touch",
    )(value, token)


def combine(kernel, shapes, place, values, scratch=(), tokens=()):
    vmem = pl.BlockSpec(memory_space=pltpu.VMEM)
    return pl.pallas_call(
        kernel,
        in_specs=[pl.BlockSpec(memory_space=pltpu.SMEM)]
        + [vmem] * (len(values) + len(tokens)),
        out_specs=[vmem] * len(shapes),
        out_shape=[jax.ShapeDtypeStruct(*shape) for shape in shapes],
        scratch_shapes=list(scratch),
        compiler_params=pltpu.CompilerParams(vmem_limit_bytes=24 * MIB),
        cost_estimate=pl.CostEstimate(flops=0, bytes_accessed=MIB, transcendentals=0),
        name=kernel.__name__,
    )(place, *values, *tokens)


def along_major(value, by):
    return fetch(value, lambda x, c, y, z: (x, c, y - by, z) if c else (x - by, c, y, z))


def along_other(value, by):
    return fetch(value, lambda x, c, y, z: (x - by, c, y, z) if c else (x, c, y - by, z))


def along_z(value, by):
    return fetch(value, lambda x, c, y, z: (x, c, y, z - by))


def exchange(values, along):
    return [values[0]] + [along(values[by], by) for by in (1, 2, 3)]


def first_sums(place, partial, latent_grad, gathered, token):
    sums = exchange(partial, along_major)
    input_grad, token = input_grads(latent_grad, gathered, token)
    token = touch(sums[1], touch(sums[2], token))
    outs = [((960, 128), bf16)] * 4
    return combine(first_kernel, outs, place, sums, tokens=[token]), input_grad


def last_sums(place, sums):
    sums = exchange(sums, along_other)
    scratch = [pltpu.VMEM((4, 64, 128), f32)]
    sums = combine(second_kernel, [((240, 128), bf16)] * 4, place, sums, scratch)
    sums = exchange(sums, along_z)
    return combine(third_kernel, [((56, 512), f32), ((4, 128), f32)], place, sums)


def shards(inputs, cotangent, weight, norm_gain):
    dp, shard = lax.axis_index("dp"), lax.axis_index("shard")
    core = dp % 2
    place = jnp.stack([dp // 2, core, shard // 4, shard % 4]).astype(jnp.int32)
    half = lax.dynamic_slice_in_dim(weight, core * 256, 256, 1)
    other_inputs = twin(inputs)
    kept, token = turn(place, inputs)
    line = join([half] + [fetch_first(half, by) for by in (1, 2, 3)], token)
    mine = [line] + [fetch_second(line, by) for by in (1, 2, 3)]
    other, token = turn(place, other_inputs)
    gain = norm_gain.reshape(1, 512)
    parts_of = functools.partial(latent_part, place, inputs)
    theirs = {0: twin(line)}
    first, _ = parts_of(mine[0], 0, 0)
    second, done = parts_of(theirs[0], 1, 0)
    mine[1] = tie(mine[1], token, done)
    theirs[1] = twin(mine[1])
    theirs[3] = twin(mine[3])
    first, _ = parts_of(mine[1], 0, 1, first)
    first, done = parts_of(mine[3], 0, 3, first)
    second, _ = parts_of(theirs[1], 1, 1, second)
    second, after = parts_of(theirs[3], 1, 3, second)
    mine[2] = tie(mine[2], done, after)
    theirs[2] = twin(mine[2])
    first, _ = parts_of(mine[2], 0, 2, first)
    second, _ = parts_of(theirs[2], 1, 2, second, (first, cotangent, gain))
    theirs = [theirs[i] for i in four]
    latent_grad = second
    other_grad = twin(latent_grad)
    partial, tokens = [None] * 4, []
    for by in (2, 1, 3, 0):
        partial[by], token = weight_grads(place, kept, other, latent_grad, other_grad, by, tokens)
        tokens = [token]
    gathered = assemble(place, mine + theirs, token)
    sums, input_grad = first_sums(place, partial, latent_grad, gathered, token)
    weight_grad, gain_grad = last_sums(place, sums)
    return (input_grad, weight_grad, gain_grad.reshape(512))


def solution(mesh):
    placed = (P(("dp", "shard"), None), P(("dp", "shard"), None), P("shard", None), P())
    return jax.shard_map(
        shards,
        mesh=mesh,
        in_specs=placed,
        out_specs=(P(("dp", "shard"), None), P(("dp", "shard"), None), P()),
        check_vma=False,
    )
```
